32 devices in a mesh: freq: 8 (over y, x, core), blk: 4 (over z).
Axes of the slice: x: 2, y: 2, z: 4, core: 2. Of those that a mesh axis runs over, the one named last changes fastest.
Arguments:
- traces: bfloat16 [32, 4096, 1024], P(('blk', 'freq')), may hold values from -6 to 6
- fir: float32 [128], replicated, may hold values from -0.5 to 0.5
- targets: int32 [256], replicated, may hold values from 0 to 31
- band: int32 [2], replicated, may hold values from 1 to 512, as said below
Outputs:
- multiples: float32 [32, 2, 256, 4096], P('freq', None, None, 'blk')
The draws below stay inside these ranges and needn't reach their ends.
Inputs may be any that keep to these rules, and one draw needn't show every extreme that they name: band[1] is 512 and band[1] - band[0] is at least 256.
All inputs are finite; a program needn't handle non-finite values.
Results may differ from the reference program's by a relative error of at most 0.019.
Values may be sent and summed in bfloat16 or wider, within the bound.
A program may use at most 128 MiB of HBM per device.

```python
import math
import jax
import jax.numpy as jnp
from jax import lax

NR = 4096
NT = 1024
TAPS = 128
TARGETS = 256
NS = 32
NF = 32
STRIDE = 128


def draw_band(key, part):
    band_high = jnp.asarray(NT // 2, jnp.int32)
    band_low = jax.random.randint(key, (), 1, NT // 4 + 1)
    return jnp.stack([band_low, band_high]).astype(jnp.int32)


def touch_ends(entries, rng, low, high):
    longest = entries.shape.index(max(entries.shape))
    spots = []
    for shift in (0, 1):
        where = [jax.random.randint(jax.random.fold_in(rng, axis), (), 0, length) for axis, length in enumerate(entries.shape)]
        where[longest] = (where[longest] + shift) % entries.shape[longest]
        spots.append(tuple(where))
    return entries.at[spots[0]].set(low).at[spots[1]].set(high)


def level_of(rng, dims, pieces, low, top_value):
    def one(axis_at, shards_of):
        steps = jax.random.uniform(jax.random.fold_in(jax.random.fold_in(rng, 6), axis_at), (shards_of,), jnp.float32, low / len(pieces), top_value / len(pieces))
        return jnp.repeat(jnp.exp(steps), dims[axis_at] // shards_of).reshape((-1,) + (1,) * (len(dims) - axis_at - 1))

    level = one(*pieces[0])
    for cut in pieces[1:]:
        level = level * one(*cut)
    return level


def centred(own_key, extent, deviation, reach, shards=(), kind=jnp.bfloat16):
    loudness = level_of(own_key, extent, shards, -0.22, 0.18) if shards else 1.0
    drawn = jax.random.normal(own_key, extent, jnp.float32) * deviation * loudness
    return jnp.minimum(jnp.maximum(drawn, -reach), reach).astype(kind)


def setup_inputs(seed: int = 0) -> dict:
    arg_keys = jax.random.split(jax.random.key(seed), 5)
    return {
        "traces": centred(arg_keys[0], (NS, NR, NT), 1.0, 6.0, ((0, 32),)),
        "fir": centred(arg_keys[1], (TAPS,), TAPS ** -0.5, 0.5, (), jnp.float32),
        "targets": touch_ends(jax.random.randint(arg_keys[2], (TARGETS,), 0, NS), jax.random.fold_in(arg_keys[2], 1), 0, NS - 1).astype(jnp.int32),
        "band": draw_band(jax.random.fold_in(arg_keys[4], 71), 0),
    }


def phase_table(band, freq_count, time_count):
    band_low = band[0]
    band_high = band[1]
    freq_index = jnp.arange(freq_count, dtype=jnp.int32)
    numerator = band_low * freq_count + (band_high - band_low) * freq_index
    time_index = jnp.arange(time_count, dtype=jnp.int32)
    turn_count = jnp.mod(time_index[:, None] * numerator[None, :], freq_count * time_count)
    phase_angle = turn_count.astype(jnp.float32) * (2.0 * math.pi / (freq_count * time_count))
    table = jnp.stack([jnp.cos(phase_angle), -jnp.sin(phase_angle)], axis=2) * (1.0 / math.sqrt(time_count))
    return table.reshape(time_count, 2 * freq_count)

def shaping_matrix(fir, time_count, tap_count):
    time_index = jnp.arange(time_count, dtype=jnp.int32)
    lag_table = time_index[None, :] - time_index[:, None]
    inside = (lag_table >= 0) & (lag_table < tap_count)
    values = fir[jnp.clip(lag_table, 0, tap_count - 1)]
    return jnp.where(inside, values, 0.0)

def reference(traces, fir, targets, band):
    dft_table = phase_table(band, NF, NT)
    mixed_table = jnp.dot(shaping_matrix(fir, NT, TAPS), dft_table, precision=lax.Precision.HIGHEST)

    def one_shot(shot_trace):
        out_rows = jnp.einsum('tc,rt->cr', mixed_table, shot_trace.astype(jnp.float32), precision=lax.Precision.HIGHEST)
        return out_rows.astype(jnp.bfloat16)
    spectrum = lax.map(one_shot, traces)
    spectrum = spectrum.reshape(NS, NF, 2, NR).transpose(1, 2, 0, 3)
    picked = jnp.take(spectrum, targets, axis=2)[..., ::STRIDE]
    chosen = jnp.swapaxes(picked, 2, 3)
    weight_scale = 1.0 / math.sqrt(NS)

    def one_freq(both_parts):
        target_rows, shot_rows = both_parts
        real_part = target_rows[0].astype(jnp.float32)
        imag_part = target_rows[1].astype(jnp.float32)
        left_block = jnp.stack([jnp.concatenate([real_part, -imag_part], 0), jnp.concatenate([imag_part, real_part], 0)])
        right_block = shot_rows.astype(jnp.float32).reshape(2 * NS, NR)
        return jnp.einsum('ojk,jr->okr', left_block, right_block, precision=lax.Precision.HIGHEST) * weight_scale
    return lax.map(one_freq, (chosen, spectrum))
```

```python
import functools
import math

import jax
import jax.numpy as jnp
from jax import lax
from jax.experimental import pallas as pl
from jax.experimental.pallas import tpu as pltpu
from jax.sharding import PartitionSpec as P

FREQ_DEV = 4
PARTS = 2 * FREQ_DEV
ROWS = 2 * PARTS
VMEM_LIMIT = 40 * 2**20
GROUP = 32
MESH = pl.DeviceIdType.MESH


def dot(a, b, dims=(((1,), (0,)), ((), ())), precision=None):
    return lax.dot_general(a, b, dims, precision=precision, preferred_element_type=jnp.float32)


def cos_turns(turns):
    w = (0.25 - jnp.abs(turns - 0.5)) * (2.0 * math.pi)
    w2 = w * w
    total = jnp.full_like(w, 1.0 / math.factorial(13))
    for order in (11, 9, 7, 5, 3, 1):
        sign = 1.0 if order % 4 == 1 else -1.0
        total = total * w2 + sign / math.factorial(order)
    return -(total * w)


def flipped(index, offset, count):
    total = 0
    bit = 1
    while bit < count:
        total = total + bit * lax.rem(index // bit + (offset // bit) % 2, 2)
        bit *= 2
    return total


def send_kernel(
    freq_devs, blk_devs, col_stride,
    band_hbm, fir_hbm, targets_hbm, traces_ref, recv_ref, left_ref, sort_ref,
    band_ref, fir_ref, targets_ref,
    traces_buf, spots_buf, table, outgoing, near_out, near_in, plane_out, plane_ref,
    small_sem, chunk_sem, spot_sem, own_sem, send_sem, recv_sem,
    near_send, near_recv, plane_own, plane_send, plane_recv,
):
    me_f = lax.axis_index("freq")
    me_b = lax.axis_index("blk")
    me = me_b * freq_devs + me_f
    n = freq_devs * blk_devs
    spots, _, time_count = traces_buf.shape
    rec_count = spots * col_stride
    width = rec_count // blk_devs
    half = width // 2
    freq_count = FREQ_DEV * freq_devs
    cols = 2 * freq_count
    taps = fir_ref.shape[1]
    per = width // col_stride
    _, near_rows, near_lanes = near_out.shape
    packed = near_lanes // spots

    crossing = list(range(blk_devs // 2, blk_devs))
    offsets = crossing + list(range(blk_devs // 2 - 1, -1, -1))

    def spot_copy():
        return pltpu.make_async_copy(
            traces_ref.at[:, pl.ds(0, 16), :], spots_buf, spot_sem
        )

    def chunk_copy(step):
        block = flipped(me_b, offsets[step], blk_devs)
        return pltpu.make_async_copy(
            traces_ref.at[pl.ds(block * per, per)],
            traces_buf.at[pl.ds(step * per, per)],
            chunk_sem.at[step],
        )

    small = [
        pltpu.make_async_copy(band_hbm, band_ref, small_sem.at[0]),
        pltpu.make_async_copy(fir_hbm, fir_ref, small_sem.at[1]),
        pltpu.make_async_copy(targets_hbm, targets_ref, small_sem.at[2]),
    ]
    small[0].start()
    chunk_copy(0).start()
    barrier = pltpu.get_barrier_semaphore()

    @pl.loop(1, n)
    def _(d):
        to = lax.rem(me + d, n)
        pl.semaphore_signal(
            barrier, inc=1, device_id=(lax.rem(to, freq_devs), to // freq_devs), device_id_type=MESH
        )

    small[1].start()
    small[2].start()
    spot_copy().start()
    for step in range(1, blk_devs):
        chunk_copy(step).start()
    small[0].wait()
    small[1].wait()

    row = lax.broadcasted_iota(jnp.int32, (cols, time_count), 0)
    time = lax.broadcasted_iota(jnp.int32, (cols, time_count), 1)
    period = freq_count * time_count
    low = band_ref[0]
    high = band_ref[1]
    numerator = low * freq_count + (high - low) * (row >> 1)
    turn = numerator * time

    def cosine(shift):
        return cos_turns(((turn + shift) & (period - 1)).astype(jnp.float32) * (1.0 / period))

    quarter = period // 4
    part = (row & 1) * quarter
    cos_full = cosine(part)
    sin_full = cosine(part + 3 * quarter)
    head = turn[:, :taps]
    lag = lax.broadcasted_iota(jnp.int32, (taps, taps), 0)
    late = lax.broadcasted_iota(jnp.int32, (taps, taps), 1)
    kept = jnp.where(lag < taps - late, 1.0, 0.0).astype(jnp.float32)
    fir = fir_ref[...]
    scale = 1.0 / math.sqrt(time_count)

    def head_cos(shift):
        return cos_turns(((head + shift) & (period - 1)).astype(jnp.float32) * (1.0 / period))

    sum_cos = dot(head_cos(0) * fir, kept, precision=lax.Precision.HIGHEST) * scale
    sum_sin = dot(head_cos(3 * quarter) * fir, kept, precision=lax.Precision.HIGHEST) * scale
    body = time_count - taps
    mixed = jnp.concatenate(
        [
            cos_full[:, :body] * sum_cos[:, :1] - sin_full[:, :body] * sum_sin[:, :1],
            cos_full[:, body:] * sum_cos - sin_full[:, body:] * sum_sin,
        ],
        1,
    )
    mixed_high = mixed.astype(jnp.bfloat16)
    mixed_low = mixed - mixed_high.astype(jnp.float32)
    table[...] = (
        jnp.concatenate([mixed_high.astype(jnp.float32), mixed_low], 0).T.astype(jnp.bfloat16)
    )

    def spectrum_of(rows):
        both = dot(rows, table[...]).T
        return both[:cols] + both[cols:]


    def near_copy(f, slot):
        return pltpu.make_async_remote_copy(
            src_ref=near_out.at[f],
            dst_ref=near_in.at[slot],
            send_sem=near_send.at[f],
            recv_sem=near_recv.at[slot],
            device_id=(f, me_b),
            device_id_type=MESH,
        )

    def plane_copy(offset, slot):
        return pltpu.make_async_remote_copy(
            src_ref=plane_out,
            dst_ref=plane_ref.at[slot],
            send_sem=plane_send.at[offset],
            recv_sem=plane_recv.at[slot],
            device_id=(me_f, flipped(me_b, offset, blk_devs)),
            device_id_type=MESH,
        )

    own_plane = pltpu.make_async_copy(plane_out, plane_ref.at[me_b], plane_own)

    def remote(step, f):
        block = flipped(me_b, offsets[step], blk_devs)
        return pltpu.make_async_remote_copy(
            src_ref=outgoing.at[step, f],
            dst_ref=recv_ref.at[me],
            send_sem=send_sem.at[step * freq_devs + f],
            recv_sem=recv_sem.at[me],
            device_id=(f, block),
            device_id_type=MESH,
        )

    own = pltpu.make_async_copy(outgoing.at[blk_devs - 1, me_f], recv_ref.at[me], own_sem)
    for step in range(blk_devs):
        chunk_copy(step).wait()
        values = spectrum_of(
            traces_buf[pl.ds(step * per, per)].reshape(width, time_count)
        )
        values = values.reshape(freq_devs, PARTS, width)
        values = jnp.concatenate([values[:, :, :half], values[:, :, half:]], 1)
        outgoing[step] = values.astype(jnp.bfloat16)
        if step == 0:
            pl.semaphore_wait(barrier, n - 1)
        first = 0
        if step == blk_devs - 1:
            own.start()
            first = 1

        @pl.loop(first, freq_devs)
        def _(d):
            remote(step, lax.rem(me_f + d, freq_devs)).start()

        if step == 0:
            spot_copy().wait()
            near = spectrum_of(spots_buf[...].reshape(spots * 16, time_count)).astype(jnp.bfloat16)
            spot_row = lax.broadcasted_iota(jnp.int32, (spots * 16, near_lanes), 0)
            spot_col = lax.broadcasted_iota(jnp.int32, (spots * 16, near_lanes), 1)
            shift = lax.rem(me_f, packed) * spots
            pick = jnp.where(spot_row == (spot_col - shift) * 16, 1.0, 0.0).astype(jnp.bfloat16)
            at_spots = dot(near, pick).reshape(freq_devs, PARTS, near_lanes)
            at_spots = jnp.concatenate([at_spots] * (near_rows // PARTS), 1)
            line = lax.broadcasted_iota(jnp.int32, at_spots.shape, 1) // PARTS
            near_out[...] = jnp.where(line == me_f // packed, at_spots, 0.0).astype(jnp.bfloat16)

            @pl.loop(1, freq_devs)
            def _(d):
                near_copy(lax.rem(me_f + d, freq_devs), me_f).start()

        if step == blk_devs - 2:
            total = near_out[me_f].astype(jnp.float32)
            for d in range(1, freq_devs):
                source = lax.rem(me_f + d, freq_devs)
                near_copy(source, source).wait_recv()
                total = total + near_in[source].astype(jnp.float32)
            plane_out[...] = total.astype(jnp.bfloat16)
            own_plane.start()
            for offset in range(1, blk_devs):
                plane_copy(offset, me_b).start()

    rows = recv_ref.shape[1]
    fill_sort(sort_ref, rows)
    own_plane.wait()
    for offset in range(1, blk_devs):
        plane_copy(offset, flipped(me_b, offset, blk_devs)).wait_recv()
    small[2].wait()
    fill_left(freq_devs, targets_ref, plane_ref, left_ref)
    own.wait()

    @pl.loop(1, freq_devs)
    def _(d):
        near_copy(lax.rem(me_f + d, freq_devs), me_f).wait_send()

    for offset in range(1, blk_devs):
        plane_copy(offset, me_b).wait_send()
    for step in range(blk_devs):

        @pl.loop(1 if step == blk_devs - 1 else 0, freq_devs)
        def _(d):
            remote(step, lax.rem(me_f + d, freq_devs)).wait_send()

    @pl.loop(1, n)
    def _(d):
        source = lax.rem(me + d, n)
        pltpu.make_async_remote_copy(
            src_ref=outgoing.at[0, 0],
            dst_ref=recv_ref.at[source],
            send_sem=send_sem.at[0],
            recv_sem=recv_sem.at[source],
            device_id=(lax.rem(source, freq_devs), source // freq_devs),
            device_id_type=MESH,
        ).wait_recv()


def fill_sort(sort_ref, rows):
    lines, depth = sort_ref.shape
    half = rows // 2
    line = lax.broadcasted_iota(jnp.int32, (lines, depth), 0)
    place = lax.broadcasted_iota(jnp.int32, (lines, depth), 1)
    group = line // GROUP
    home = (line % GROUP) * rows + (group // 2) % 2 * half + group // 4 * 2 + group % 2
    sort_ref[...] = jnp.where(place == home, 1.0, 0.0).astype(jnp.bfloat16)


def fill_left(freq_devs, targets_ref, plane_ref, left_ref):
    blk_devs, near_rows, near_lanes = plane_ref.shape
    shots = left_ref.shape[2] // 2
    packed = near_lanes // shots
    count = targets_ref.shape[1]
    wide = max(128, 2 * shots)
    wanted = jnp.broadcast_to(targets_ref[...].astype(jnp.float32), (128, count)).T
    shot = lax.broadcasted_iota(jnp.int32, (count, 2 * shots), 1)
    shot = jnp.where(shot >= shots, shot - shots, shot)
    chooser = jnp.where(shot == wanted[:, :1].astype(jnp.int32), 1.0, 0.0).astype(jnp.bfloat16)
    fold_row = lax.broadcasted_iota(jnp.int32, (near_lanes, wide), 0)
    fold_col = lax.broadcasted_iota(jnp.int32, (near_lanes, wide), 1)
    fold_spot = fold_col // (2 * GROUP) * GROUP + fold_col % GROUP
    fold = jnp.where(fold_row % shots == fold_spot % shots, 1.0, 0.0).astype(jnp.bfloat16)
    near_depth = blk_devs * near_rows
    for i in range(FREQ_DEV):
        line = lax.broadcasted_iota(jnp.int32, (2 * shots, near_depth), 0)
        place = lax.broadcasted_iota(jnp.int32, (2 * shots, near_depth), 1)
        part = line // shots
        from_shot = line - part * shots
        from_f = from_shot % freq_devs
        home = (from_shot // freq_devs) * near_rows + (from_f // packed) * PARTS + 2 * i + part
        pick = jnp.where(place == home, 1.0, 0.0).astype(jnp.bfloat16)
        near = dot(pick, plane_ref[...].reshape(near_depth, near_lanes))
        slot = lax.broadcasted_iota(jnp.int32, near.shape, 0) % freq_devs % packed
        lane = lax.broadcasted_iota(jnp.int32, near.shape, 1)
        near = jnp.where(lane // shots == slot, near, 0.0).astype(jnp.bfloat16)
        near = dot(near, fold)
        source = lax.broadcasted_iota(jnp.int32, near.shape, 0) >= shots
        lane = lax.broadcasted_iota(jnp.int32, near.shape, 1)
        target = lane // GROUP % 2 == 1
        inside = lane < 2 * shots
        same = inside & (source == target)
        other = inside & (source != target)
        parts = [
            jnp.where(same, jnp.where(source, -near, near), 0.0),
            jnp.where(other, near, 0.0),
        ]
        for o in range(2):
            left = dot(chooser, parts[o].astype(jnp.bfloat16)).astype(jnp.bfloat16)
            left_ref[i, pl.ds(o * count, count), :] = left[:, : 2 * shots]


def product_kernel(recv_ref, left_ref, sort_ref, out_ref, made, sems):
    shots, rows, half = recv_ref.shape
    count = left_ref.shape[1] // 2
    span = GROUP * rows
    scale = 1.0 / math.sqrt(shots)

    def write(i, o):
        return pltpu.make_async_copy(
            made.at[i, pl.ds(o * count, count)], out_ref.at[i, o], sems.at[i, o]
        )

    for i in range(FREQ_DEV):
        lines = sort_ref[pl.ds(i * 4 * GROUP, 4 * GROUP), :]
        rights = [
            dot(lines, recv_ref[pl.ds(g * GROUP, GROUP)].reshape(span, half)).astype(jnp.bfloat16)
            for g in range(shots // GROUP)
        ]
        rights = [
            jnp.concatenate([r[2 * GROUP * h : 2 * GROUP * (h + 1)] for r in rights], 0)
            for h in range(2)
        ]
        for o in range(2):
            left = left_ref[i, pl.ds(o * count, count), :]
            for h in range(2):
                made[i, pl.ds(o * count, count), pl.ds(h * half, half)] = dot(left, rights[h]) * scale
            write(i, o).start()

    for i in range(FREQ_DEV):
        for o in range(2):
            write(i, o).wait()


def per_device(traces, fir, targets, band):
    shot_dev, rec_count, time_count = traces.shape
    freq_devs = lax.axis_size("freq")
    blk_devs = lax.axis_size("blk")
    n = freq_devs * blk_devs
    assert shot_dev == 1
    assert blk_devs & (blk_devs - 1) == 0
    col_stride = rec_count // n
    width = rec_count // blk_devs
    half = width // 2
    lanes = half
    near_lanes = max(128, n)
    packed = near_lanes // n
    near_rows = freq_devs // packed * PARTS
    cols = 2 * FREQ_DEV * freq_devs
    count = targets.shape[0]
    assert n % GROUP == 0
    lines = 4 * FREQ_DEV * GROUP
    hbm = lambda x: pltpu.with_memory_space_constraint(x, pltpu.HBM)
    received, lefts, sorter = pl.pallas_call(
        functools.partial(send_kernel, freq_devs, blk_devs, col_stride),
        out_shape=[
            pltpu.VMEM((n, ROWS, lanes), jnp.bfloat16),
            pltpu.VMEM((FREQ_DEV, 2 * count, 2 * n), jnp.bfloat16),
            pltpu.VMEM((lines, GROUP * ROWS), jnp.bfloat16),
        ],
        in_specs=[pl.BlockSpec(memory_space=pl.ANY)] * 4,
        out_specs=[pl.BlockSpec(memory_space=pltpu.VMEM)] * 3,
        scratch_shapes=[
            pltpu.SMEM((2,), jnp.int32),
            pltpu.VMEM((1, fir.shape[0]), jnp.float32),
            pltpu.VMEM((1, count), jnp.int32),
            pltpu.VMEM((n, col_stride, time_count), jnp.bfloat16),
            pltpu.VMEM((n, 16, time_count), jnp.bfloat16),
            pltpu.VMEM((time_count, 2 * cols), jnp.bfloat16),
            pltpu.VMEM((blk_devs, freq_devs, ROWS, lanes), jnp.bfloat16),
            pltpu.VMEM((freq_devs, near_rows, near_lanes), jnp.bfloat16),
            pltpu.VMEM((freq_devs, near_rows, near_lanes), jnp.bfloat16),
            pltpu.VMEM((near_rows, near_lanes), jnp.bfloat16),
            pltpu.VMEM((blk_devs, near_rows, near_lanes), jnp.bfloat16),
            pltpu.SemaphoreType.DMA((3,)),
            pltpu.SemaphoreType.DMA((blk_devs,)),
            pltpu.SemaphoreType.DMA,
            pltpu.SemaphoreType.DMA,
            pltpu.SemaphoreType.DMA((n,)),
            pltpu.SemaphoreType.DMA((n,)),
            pltpu.SemaphoreType.DMA((freq_devs,)),
            pltpu.SemaphoreType.DMA((freq_devs,)),
            pltpu.SemaphoreType.DMA,
            pltpu.SemaphoreType.DMA((blk_devs,)),
            pltpu.SemaphoreType.DMA((blk_devs,)),
        ],
        compiler_params=pltpu.CompilerParams(
            collective_id=0, has_side_effects=True, vmem_limit_bytes=VMEM_LIMIT
        ),
    )(
        hbm(band),
        hbm(fir.reshape(1, -1)),
        hbm(targets.reshape(1, -1)),
        hbm(traces.reshape(n, col_stride, time_count)),
    )
    return pl.pallas_call(
        product_kernel,
        out_shape=jax.ShapeDtypeStruct((FREQ_DEV, 2, count, width), jnp.float32),
        in_specs=[pl.BlockSpec(memory_space=pltpu.VMEM)] * 3,
        out_specs=pl.BlockSpec(memory_space=pl.ANY),
        scratch_shapes=[
            pltpu.VMEM((FREQ_DEV, 2 * count, width), jnp.float32),
            pltpu.SemaphoreType.DMA((FREQ_DEV, 2)),
        ],
        compiler_params=pltpu.CompilerParams(vmem_limit_bytes=VMEM_LIMIT),
    )(received, lefts, sorter)


def solution(mesh):
    placed = (P(("blk", "freq"), None, None), P(), P(), P())
    return jax.shard_map(
        per_device,
        mesh=mesh,
        in_specs=placed,
        out_specs=P("freq", None, None, "blk"),
        check_vma=False,
    )
```

```python
import functools
import math

import jax
import jax.numpy as jnp
from jax import lax
from jax.experimental import pallas as pl
from jax.experimental.pallas import tpu as pltpu
from jax.sharding import PartitionSpec as P

FREQ_DEV = 4
PARTS = 2 * FREQ_DEV
ROWS = 2 * PARTS
VMEM_LIMIT = 40 * 2**20
GROUP = 32
MESH = pl.DeviceIdType.MESH


def dot(a, b, dims=(((1,), (0,)), ((), ())), precision=None):
    return lax.dot_general(a, b, dims, precision=precision, preferred_element_type=jnp.float32)


def cos_turns(turns):
    w = (0.25 - jnp.abs(turns - 0.5)) * (2.0 * math.pi)
    w2 = w * w
    total = jnp.full_like(w, 1.0 / math.factorial(13))
    for order in (11, 9, 7, 5, 3, 1):
        sign = 1.0 if order % 4 == 1 else -1.0
        total = total * w2 + sign / math.factorial(order)
    return -(total * w)


def flipped(index, offset, count):
    total = 0
    bit = 1
    while bit < count:
        total = total + bit * lax.rem(index // bit + (offset // bit) % 2, 2)
        bit *= 2
    return total


def send_kernel(
    freq_devs, blk_devs, col_stride,
    band_hbm, fir_hbm, targets_hbm, traces_ref, recv_ref, left_ref, sort_ref,
    band_ref, fir_ref, targets_ref,
    traces_buf, spots_buf, table, outgoing, near_out, near_in, plane_out, plane_ref,
    small_sem, chunk_sem, spot_sem, send_sem, recv_sem,
    near_send, near_recv, plane_send, plane_recv,
):
    me_f = lax.axis_index("freq")
    me_b = lax.axis_index("blk")
    me = me_b * freq_devs + me_f
    n = freq_devs * blk_devs
    spots, _, time_count = traces_buf.shape
    rec_count = spots * col_stride
    width = rec_count // blk_devs
    half = width // 2
    freq_count = FREQ_DEV * freq_devs
    cols = 2 * freq_count
    per = width // col_stride
    _, near_rows, near_lanes = near_out.shape
    packed = near_lanes // spots

    crossing = list(range(blk_devs // 2, blk_devs))
    offsets = crossing + list(range(blk_devs // 2 - 1, -1, -1))

    def spot_copy():
        return pltpu.make_async_copy(
            traces_ref.at[:, pl.ds(0, 16), :], spots_buf, spot_sem
        )

    def chunk_copy(step):
        block = flipped(me_b, offsets[step], blk_devs)
        return pltpu.make_async_copy(
            traces_ref.at[pl.ds(block * per, per)],
            traces_buf.at[pl.ds(step * per, per)],
            chunk_sem.at[step],
        )

    def enter(d):
        to = lax.rem(me + d, n)
        pl.semaphore_signal(
            barrier, inc=1, device_id=(lax.rem(to, freq_devs), to // freq_devs), device_id_type=MESH
        )

    def near_copy(f):
        return pltpu.make_async_remote_copy(
            src_ref=near_out.at[f],
            dst_ref=near_in.at[me_f],
            send_sem=near_send,
            recv_sem=near_recv,
            device_id=(f, me_b),
            device_id_type=MESH,
        )

    def plane_copy(offset, slot):
        return pltpu.make_async_remote_copy(
            src_ref=plane_out,
            dst_ref=plane_ref.at[slot],
            send_sem=plane_send,
            recv_sem=plane_recv,
            device_id=(me_f, flipped(me_b, offset, blk_devs)),
            device_id_type=MESH,
        )

    def remote(step, f):
        block = flipped(me_b, offsets[step], blk_devs)
        return pltpu.make_async_remote_copy(
            src_ref=outgoing.at[step, f],
            dst_ref=recv_ref.at[me],
            send_sem=send_sem.at[step],
            recv_sem=recv_sem,
            device_id=(f, block),
            device_id_type=MESH,
        )

    def arrived(ref, sem):
        pltpu.make_async_copy(ref, ref, sem).wait()

    small = [
        pltpu.make_async_copy(band_hbm, band_ref, small_sem.at[0]),
        pltpu.make_async_copy(fir_hbm, fir_ref, small_sem.at[1]),
        pltpu.make_async_copy(targets_hbm, targets_ref, small_sem.at[2]),
    ]
    barrier = pltpu.get_barrier_semaphore()
    with jax.named_scope("signals"):
        small[0].start()
        small[1].start()
        spot_copy().start()
        pl.loop(1, n)(enter)
    for step in range(blk_devs):
        chunk_copy(step).start()
    small[2].start()
    with jax.named_scope("small_wait"):
        small[0].wait()
        small[1].wait()
    with jax.named_scope("table"):
        fill_table(band_ref, fir_ref, table, freq_count)

    def spectrum_of(rows):
        both = dot(table[...], rows, (((1,), (1,)), ((), ())))
        return both[:cols] + both[cols:]

    with jax.named_scope("spots"):
        spot_copy().wait()
        near = spectrum_of(spots_buf[...].reshape(spots * 16, time_count)).astype(jnp.bfloat16)
        spot_row = lax.broadcasted_iota(jnp.int32, (spots * 16, near_lanes), 0)
        spot_col = lax.broadcasted_iota(jnp.int32, (spots * 16, near_lanes), 1)
        shift = lax.rem(me_f, packed) * spots
        pick = jnp.where(spot_row == (spot_col - shift) * 16, 1.0, 0.0).astype(jnp.bfloat16)
        at_spots = dot(near, pick).reshape(freq_devs, PARTS, near_lanes)
        at_spots = jnp.concatenate([at_spots] * (near_rows // PARTS), 1)
        line = lax.broadcasted_iota(jnp.int32, at_spots.shape, 1) // PARTS
        near_out[...] = jnp.where(line == me_f // packed, at_spots, 0.0).astype(jnp.bfloat16)
        near_in[me_f] = near_out[me_f]

    for step in range(blk_devs):
        with jax.named_scope(f"chunk{step}"):
            chunk_copy(step).wait()
            values = spectrum_of(traces_buf[pl.ds(step * per, per)].reshape(width, time_count))
            values = values.reshape(freq_devs, PARTS, width)
            values = jnp.concatenate([values[:, :, :half], values[:, :, half:]], 1)
            outgoing[step] = values.astype(jnp.bfloat16)
        if step == 0:
            with jax.named_scope("barrier"):
                pl.semaphore_wait(barrier, n - 1)

            @pl.loop(1, freq_devs)
            def _(d):
                near_copy(lax.rem(me_f + d, freq_devs)).start()

        if step == 1:
            with jax.named_scope("plane"):
                arrived(near_in.at[pl.ds(0, freq_devs - 1)], near_recv)
                total = near_in[...].astype(jnp.float32)
                plane_out[...] = jnp.sum(total, 0).astype(jnp.bfloat16)
                plane_ref[me_b] = plane_out[...]
            for offset in range(1, blk_devs):
                plane_copy(offset, me_b).start()

        first = 0
        if step == blk_devs - 1:
            recv_ref[me] = outgoing[step, me_f]
            first = 1

        with jax.named_scope("send"):

            @pl.loop(first, freq_devs)
            def _(d):
                remote(step, lax.rem(me_f + d, freq_devs)).start()

    with jax.named_scope("sort"):
        fill_sort(sort_ref, recv_ref.shape[1])
    with jax.named_scope("plane_wait"):
        arrived(plane_ref.at[pl.ds(0, blk_devs - 1)], plane_recv)
        small[2].wait()
    with jax.named_scope("left"):
        fill_left(freq_devs, targets_ref, plane_ref, left_ref)
    with jax.named_scope("send_wait"):
        arrived(near_in.at[pl.ds(0, freq_devs - 1)], near_send)
        arrived(plane_ref.at[pl.ds(0, blk_devs - 1)], plane_send)
        for step in range(blk_devs - 1):
            arrived(outgoing.at[step], send_sem.at[step])
        arrived(outgoing.at[blk_devs - 1, pl.ds(0, freq_devs - 1)], send_sem.at[blk_devs - 1])
    with jax.named_scope("recv_wait"):
        arrived(recv_ref.at[pl.ds(0, n - 1)], recv_sem)


def fill_table(band_ref, fir_ref, table, freq_count):
    cols = table.shape[0] // 2
    time_count = table.shape[1]
    taps = fir_ref.shape[1]
    period = freq_count * time_count
    quarter = period // 4
    row = lax.broadcasted_iota(jnp.int32, (cols, taps), 0)
    time = lax.broadcasted_iota(jnp.int32, (cols, taps), 1)
    low = band_ref[0]
    high = band_ref[1]
    numerator = low * freq_count + (high - low) * (row >> 1)

    def cosine(turn):
        return cos_turns((turn & (period - 1)).astype(jnp.float32) * (1.0 / period))

    turn = numerator * time
    cos_in = cosine(turn)
    sin_in = cosine(turn + 3 * quarter)
    step = numerator * taps
    cos_step = cosine(step)
    sin_step = cosine(step + 3 * quarter)
    last = turn + numerator * (time_count - taps) + (row & 1) * quarter
    cos_last = cosine(last)
    sin_last = cosine(last + 3 * quarter)
    lag = lax.broadcasted_iota(jnp.int32, (taps, taps), 0)
    late = lax.broadcasted_iota(jnp.int32, (taps, taps), 1)
    kept = jnp.where(lag < taps - late, 1.0, 0.0).astype(jnp.float32)
    fir = fir_ref[...]
    weighted = jnp.concatenate([cos_in * fir, sin_in * fir], 0)
    sums = dot(weighted, kept, precision=lax.Precision.HIGHEST) * (1.0 / math.sqrt(time_count))
    sum_cos = sums[:cols]
    sum_sin = sums[cols:]
    odd = (row & 1) == 1
    cos_own = jnp.where(odd, -sin_in, cos_in)
    sin_own = jnp.where(odd, cos_in, sin_in)
    all_cos = jnp.broadcast_to(sum_cos[:, :1], (cols, taps))
    all_sin = jnp.broadcast_to(sum_sin[:, :1], (cols, taps))
    value = cos_own * all_cos - sin_own * all_sin
    other = sin_own * all_cos + cos_own * all_sin
    tiles = time_count // taps
    for tile in range(tiles):
        if tile == tiles - 1:
            value = cos_last * sum_cos - sin_last * sum_sin
        value_high = value.astype(jnp.bfloat16)
        value_low = (value - value_high.astype(jnp.float32)).astype(jnp.bfloat16)
        table[pl.ds(0, cols), pl.ds(tile * taps, taps)] = value_high
        table[pl.ds(cols, cols), pl.ds(tile * taps, taps)] = value_low
        if tile < tiles - 2:
            value, other = (
                value * cos_step - other * sin_step,
                other * cos_step + value * sin_step,
            )


def fill_sort(sort_ref, rows):
    lines, depth = sort_ref.shape
    half = rows // 2
    line = lax.broadcasted_iota(jnp.int32, (lines, depth), 0)
    place = lax.broadcasted_iota(jnp.int32, (lines, depth), 1)
    group = line // GROUP
    home = (line % GROUP) * rows + (group // 2) % 2 * half + group // 4 * 2 + group % 2
    sort_ref[...] = jnp.where(place == home, 1.0, 0.0).astype(jnp.bfloat16)


def fill_left(freq_devs, targets_ref, plane_ref, left_ref):
    blk_devs, near_rows, near_lanes = plane_ref.shape
    shots = left_ref.shape[2] // 2
    packed = near_lanes // shots
    count = targets_ref.shape[1]
    wide = max(128, 2 * shots)
    wanted = jnp.broadcast_to(targets_ref[...].astype(jnp.float32), (128, count)).T
    shot = lax.broadcasted_iota(jnp.int32, (count, 2 * shots), 1)
    shot = jnp.where(shot >= shots, shot - shots, shot)
    chooser = jnp.where(shot == wanted[:, :1].astype(jnp.int32), 1.0, 0.0).astype(jnp.bfloat16)
    fold_row = lax.broadcasted_iota(jnp.int32, (near_lanes, wide), 0)
    fold_col = lax.broadcasted_iota(jnp.int32, (near_lanes, wide), 1)
    fold_spot = fold_col // (2 * GROUP) * GROUP + fold_col % GROUP
    fold = jnp.where(fold_row % shots == fold_spot % shots, 1.0, 0.0).astype(jnp.bfloat16)
    near_depth = blk_devs * near_rows
    for i in range(FREQ_DEV):
        line = lax.broadcasted_iota(jnp.int32, (2 * shots, near_depth), 0)
        place = lax.broadcasted_iota(jnp.int32, (2 * shots, near_depth), 1)
        part = line // shots
        from_shot = line - part * shots
        from_f = from_shot % freq_devs
        home = (from_shot // freq_devs) * near_rows + (from_f // packed) * PARTS + 2 * i + part
        pick = jnp.where(place == home, 1.0, 0.0).astype(jnp.bfloat16)
        near = dot(pick, plane_ref[...].reshape(near_depth, near_lanes))
        slot = lax.broadcasted_iota(jnp.int32, near.shape, 0) % freq_devs % packed
        lane = lax.broadcasted_iota(jnp.int32, near.shape, 1)
        near = jnp.where(lane // shots == slot, near, 0.0).astype(jnp.bfloat16)
        near = dot(near, fold)
        source = lax.broadcasted_iota(jnp.int32, near.shape, 0) >= shots
        lane = lax.broadcasted_iota(jnp.int32, near.shape, 1)
        target = lane // GROUP % 2 == 1
        inside = lane < 2 * shots
        same = inside & (source == target)
        other = inside & (source != target)
        parts = [
            jnp.where(same, jnp.where(source, -near, near), 0.0),
            jnp.where(other, near, 0.0),
        ]
        for o in range(2):
            left = dot(chooser, parts[o].astype(jnp.bfloat16)).astype(jnp.bfloat16)
            left_ref[i, pl.ds(o * count, count), :] = left[:, : 2 * shots]


def product_kernel(recv_ref, left_ref, sort_ref, out_ref, made, sems):
    shots, rows, half = recv_ref.shape
    count = left_ref.shape[1] // 2
    span = GROUP * rows
    scale = 1.0 / math.sqrt(shots)

    def write(i, o):
        return pltpu.make_async_copy(
            made.at[i, pl.ds(o * count, count)], out_ref.at[i, o], sems.at[i, o]
        )

    for i in range(FREQ_DEV):
        lines = sort_ref[pl.ds(i * 4 * GROUP, 4 * GROUP), :]
        rights = [
            dot(lines, recv_ref[pl.ds(g * GROUP, GROUP)].reshape(span, half)).astype(jnp.bfloat16)
            for g in range(shots // GROUP)
        ]
        rights = [
            jnp.concatenate([r[2 * GROUP * h : 2 * GROUP * (h + 1)] for r in rights], 0)
            for h in range(2)
        ]
        for o in range(2):
            left = left_ref[i, pl.ds(o * count, count), :]
            for h in range(2):
                made[i, pl.ds(o * count, count), pl.ds(h * half, half)] = dot(left, rights[h]) * scale
            write(i, o).start()

    for i in range(FREQ_DEV):
        for o in range(2):
            write(i, o).wait()


def per_device(traces, fir, targets, band):
    shot_dev, rec_count, time_count = traces.shape
    freq_devs = lax.axis_size("freq")
    blk_devs = lax.axis_size("blk")
    n = freq_devs * blk_devs
    assert shot_dev == 1
    assert blk_devs & (blk_devs - 1) == 0
    col_stride = rec_count // n
    width = rec_count // blk_devs
    half = width // 2
    lanes = half
    near_lanes = max(128, n)
    packed = near_lanes // n
    near_rows = freq_devs // packed * PARTS
    cols = 2 * FREQ_DEV * freq_devs
    count = targets.shape[0]
    assert n % GROUP == 0
    lines = 4 * FREQ_DEV * GROUP
    hbm = lambda x: pltpu.with_memory_space_constraint(x, pltpu.HBM)
    received, lefts, sorter = pl.pallas_call(
        functools.partial(send_kernel, freq_devs, blk_devs, col_stride),
        out_shape=[
            pltpu.VMEM((n, ROWS, lanes), jnp.bfloat16),
            pltpu.VMEM((FREQ_DEV, 2 * count, 2 * n), jnp.bfloat16),
            pltpu.VMEM((lines, GROUP * ROWS), jnp.bfloat16),
        ],
        in_specs=[pl.BlockSpec(memory_space=pl.ANY)] * 4,
        out_specs=[pl.BlockSpec(memory_space=pltpu.VMEM)] * 3,
        scratch_shapes=[
            pltpu.SMEM((2,), jnp.int32),
            pltpu.VMEM((1, fir.shape[0]), jnp.float32),
            pltpu.VMEM((1, count), jnp.int32),
            pltpu.VMEM((n, col_stride, time_count), jnp.bfloat16),
            pltpu.VMEM((n, 16, time_count), jnp.bfloat16),
            pltpu.VMEM((2 * cols, time_count), jnp.bfloat16),
            pltpu.VMEM((blk_devs, freq_devs, ROWS, lanes), jnp.bfloat16),
            pltpu.VMEM((freq_devs, near_rows, near_lanes), jnp.bfloat16),
            pltpu.VMEM((freq_devs, near_rows, near_lanes), jnp.bfloat16),
            pltpu.VMEM((near_rows, near_lanes), jnp.bfloat16),
            pltpu.VMEM((blk_devs, near_rows, near_lanes), jnp.bfloat16),
            pltpu.SemaphoreType.DMA((3,)),
            pltpu.SemaphoreType.DMA((blk_devs,)),
            pltpu.SemaphoreType.DMA,
            pltpu.SemaphoreType.DMA((blk_devs,)),
            pltpu.SemaphoreType.DMA,
            pltpu.SemaphoreType.DMA,
            pltpu.SemaphoreType.DMA,
            pltpu.SemaphoreType.DMA,
            pltpu.SemaphoreType.DMA,
        ],
        compiler_params=pltpu.CompilerParams(
            collective_id=0, has_side_effects=True, vmem_limit_bytes=VMEM_LIMIT
        ),
    )(
        hbm(band),
        hbm(fir.reshape(1, -1)),
        hbm(targets.reshape(1, -1)),
        hbm(traces.reshape(n, col_stride, time_count)),
    )
    return pl.pallas_call(
        product_kernel,
        out_shape=jax.ShapeDtypeStruct((FREQ_DEV, 2, count, width), jnp.float32),
        in_specs=[pl.BlockSpec(memory_space=pltpu.VMEM)] * 3,
        out_specs=pl.BlockSpec(memory_space=pl.ANY),
        scratch_shapes=[
            pltpu.VMEM((FREQ_DEV, 2 * count, width), jnp.float32),
            pltpu.SemaphoreType.DMA((FREQ_DEV, 2)),
        ],
        compiler_params=pltpu.CompilerParams(vmem_limit_bytes=VMEM_LIMIT),
    )(received, lefts, sorter)


def solution(mesh):
    placed = (P(("blk", "freq"), None, None), P(), P(), P())
    return jax.shard_map(
        per_device,
        mesh=mesh,
        in_specs=placed,
        out_specs=P("freq", None, None, "blk"),
        check_vma=False,
    )
```

```python
import functools
import math

import jax
import jax.numpy as jnp
from jax import lax
from jax.experimental import pallas as pl
from jax.experimental.pallas import tpu as pltpu
from jax.sharding import PartitionSpec as P

FREQ_DEV = 4
PARTS = 2 * FREQ_DEV
ROWS = 2 * PARTS
VMEM_LIMIT = 40 * 2**20
VMEM_LARGE = 54 * 2**20
GROUP = 32
UNROLL = True
MESH = pl.DeviceIdType.MESH


def dot(a, b, dims=(((1,), (0,)), ((), ())), precision=None):
    return lax.dot_general(a, b, dims, precision=precision, preferred_element_type=jnp.float32)


def cos_turns(turns):
    w = (0.25 - jnp.abs(turns - 0.5)) * (2.0 * math.pi)
    w2 = w * w
    total = jnp.full_like(w, 1.0 / math.factorial(13))
    for order in (11, 9, 7, 5, 3, 1):
        sign = 1.0 if order % 4 == 1 else -1.0
        total = total * w2 + sign / math.factorial(order)
    return -(total * w)


def flipped(index, offset, count):
    total = 0
    bit = 1
    while bit < count:
        total = total + bit * lax.rem(index // bit + (offset // bit) % 2, 2)
        bit *= 2
    return total


def send_kernel(
    freq_devs, blk_devs, col_stride,
    band_hbm, fir_hbm, targets_hbm, traces_ref, recv_ref, left_ref, sort_ref,
    band_ref, fir_ref, targets_ref,
    traces_buf, spots_buf, table, outgoing, near_out, near_in, plane_out, plane_ref,
    choose, pick, inside, fold, signs,
    small_sem, chunk_sem, spot_sem, send_sem, recv_sem,
    near_send, near_recv, plane_send, plane_recv,
):
    me_f = lax.axis_index("freq")
    me_b = lax.axis_index("blk")
    me = me_b * freq_devs + me_f
    n = freq_devs * blk_devs
    spots, _, time_count = traces_buf.shape
    rec_count = spots * col_stride
    width = rec_count // blk_devs
    lanes = width // 4
    freq_count = FREQ_DEV * freq_devs
    cols = 2 * freq_count
    per = width // col_stride
    _, near_rows, near_lanes = near_out.shape
    packed = near_lanes // spots

    side = blk_devs // 2
    own_side = me_b // side
    low = 1 - own_side
    blocks = [low * side + lax.rem(low * me_b + step, side) for step in range(side)]
    blocks += [own_side * side + lax.rem(me_b + 1 + step, side) for step in range(side)]
    piece = per // 2

    def spot_copy():
        return pltpu.make_async_copy(
            traces_ref.at[:, pl.ds(0, 16), :], spots_buf, spot_sem
        )

    def chunk_copy(step, part):
        return pltpu.make_async_copy(
            traces_ref.at[pl.ds(blocks[step] * per + part * piece, piece)],
            traces_buf.at[pl.ds(step * per + part * piece, piece)],
            chunk_sem.at[step, part],
        )

    def signal_block(offset):
        block = flipped(me_b, offset, blk_devs)

        @pl.loop(0 if offset else 1, freq_devs, unroll=UNROLL)
        def _(d):
            pl.semaphore_signal(
                barrier,
                inc=1,
                device_id=(lax.rem(me_f + d, freq_devs), block),
                device_id_type=MESH,
            )

    def near_copy(f):
        return pltpu.make_async_remote_copy(
            src_ref=near_out.at[f],
            dst_ref=near_in.at[me_f],
            send_sem=near_send,
            recv_sem=near_recv,
            device_id=(f, me_b),
            device_id_type=MESH,
        )

    def plane_copy(offset, slot):
        return pltpu.make_async_remote_copy(
            src_ref=plane_out,
            dst_ref=plane_ref.at[slot],
            send_sem=plane_send,
            recv_sem=plane_recv,
            device_id=(me_f, flipped(me_b, offset, blk_devs)),
            device_id_type=MESH,
        )

    def send(step, parts):
        first = 1 if step == blk_devs - 1 else 0

        @pl.loop(first, freq_devs, unroll=UNROLL)
        def _(d):
            f = lax.rem(me_f + d, freq_devs)
            pltpu.make_async_remote_copy(
                src_ref=outgoing.at[step, f, parts],
                dst_ref=recv_ref.at[me, parts],
                send_sem=send_sem.at[step],
                recv_sem=recv_sem,
                device_id=(f, blocks[step]),
                device_id_type=MESH,
            ).start()

    def arrived(ref, sem):
        pltpu.make_async_copy(ref, ref, sem).wait()

    small = [
        pltpu.make_async_copy(band_hbm, band_ref, small_sem.at[0]),
        pltpu.make_async_copy(fir_hbm, fir_ref, small_sem.at[1]),
        pltpu.make_async_copy(targets_hbm, targets_ref, small_sem.at[2]),
    ]
    barrier = pltpu.get_barrier_semaphore()
    small[0].start()
    small[1].start()
    chunk_copy(0, 0).start()
    with jax.named_scope("signals"):
        for offset in range(blk_devs):
            signal_block(offset)
    spot_copy().start()
    with jax.named_scope("small_wait"):
        small[0].wait()
        small[1].wait()
    chunk_copy(0, 1).start()
    with jax.named_scope("table"):
        fill_table(band_ref, fir_ref, table, freq_count)

    def spectrum_of(rows):
        both = dot(table[...], rows, (((1,), (1,)), ((), ())))
        return both[:cols] + both[cols:]

    def spectra(step, part):
        with jax.named_scope(f"chunk{step}{part}"):
            chunk_copy(step, part).wait()
            rows = traces_buf[pl.ds(step * per + part * piece, piece)]
            values = spectrum_of(rows.reshape(2 * lanes, time_count))
            values = values.reshape(freq_devs, PARTS, 2 * lanes)
            values = jnp.concatenate([values[:, :, :lanes], values[:, :, lanes:]], 1)
            outgoing[step, :, part] = values.astype(jnp.bfloat16)

    chunk_copy(1, 0).start()
    small[2].start()
    spectra(0, 0)
    chunk_copy(1, 1).start()
    for step in range(2, blk_devs):
        chunk_copy(step, 0).start()
        chunk_copy(step, 1).start()
    with jax.named_scope("barrier"):
        pl.semaphore_wait(barrier, n - 1)
    send(0, pl.ds(0, 1))

    with jax.named_scope("spots"):
        spot_copy().wait()
        near = spectrum_of(spots_buf[...].reshape(spots * 16, time_count)).astype(jnp.bfloat16)
        spot_row = lax.broadcasted_iota(jnp.int32, (spots * 16, near_lanes), 0)
        spot_col = lax.broadcasted_iota(jnp.int32, (spots * 16, near_lanes), 1)
        shift = lax.rem(me_f, packed) * spots
        at_spot = jnp.where(spot_row == (spot_col - shift) * 16, 1.0, 0.0).astype(jnp.bfloat16)
        at_spots = dot(near, at_spot).reshape(freq_devs, PARTS, near_lanes)
        at_spots = jnp.concatenate([at_spots] * (near_rows // PARTS), 1)
        line = lax.broadcasted_iota(jnp.int32, at_spots.shape, 1) // PARTS
        near_out[...] = jnp.where(line == me_f // packed, at_spots, 0.0).astype(jnp.bfloat16)
        near_in[me_f] = near_out[me_f]

    @pl.loop(1, freq_devs, unroll=UNROLL)
    def _(d):
        near_copy(lax.rem(me_f + d, freq_devs)).start()

    spectra(0, 1)
    send(0, pl.ds(1, 1))
    for step in range(1, blk_devs):
        spectra(step, 0)
        spectra(step, 1)
        if step == 1:
            with jax.named_scope("plane"):
                arrived(near_in.at[pl.ds(0, freq_devs - 1)], near_recv)
                total = near_in[...].astype(jnp.float32)
                plane_out[...] = jnp.sum(total, 0).astype(jnp.bfloat16)
                plane_ref[me_b] = plane_out[...]
            for offset in range(1, blk_devs):
                plane_copy(offset, me_b).start()
        if step == blk_devs - 1:
            recv_ref[me] = outgoing[step, me_f]
        send(step, pl.ds(0, 2))

    with jax.named_scope("sort"):
        fill_sort(sort_ref, recv_ref.shape[2])
    with jax.named_scope("choice"):
        small[2].wait()
        fill_choice(freq_devs, packed, targets_ref, choose, pick, inside, fold, signs)
    with jax.named_scope("plane_wait"):
        arrived(plane_ref.at[pl.ds(0, blk_devs - 1)], plane_recv)
    with jax.named_scope("left"):
        fill_left(plane_ref, choose, pick, inside, fold, signs, left_ref)
    with jax.named_scope("send_wait"):
        arrived(near_in.at[pl.ds(0, freq_devs - 1)], near_send)
        arrived(plane_ref.at[pl.ds(0, blk_devs - 1)], plane_send)
        for step in range(blk_devs - 1):
            arrived(outgoing.at[step], send_sem.at[step])
        arrived(outgoing.at[blk_devs - 1, pl.ds(0, freq_devs - 1)], send_sem.at[blk_devs - 1])
    with jax.named_scope("recv_wait"):
        arrived(recv_ref.at[pl.ds(0, n - 1)], recv_sem)


def fill_table(band_ref, fir_ref, table, freq_count):
    cols = table.shape[0] // 2
    time_count = table.shape[1]
    taps = fir_ref.shape[1]
    period = freq_count * time_count
    quarter = period // 4
    row = lax.broadcasted_iota(jnp.int32, (cols, taps), 0)
    time = lax.broadcasted_iota(jnp.int32, (cols, taps), 1)
    low = band_ref[0]
    high = band_ref[1]
    numerator = low * freq_count + (high - low) * (row >> 1)

    def cosine(turn):
        return cos_turns((turn & (period - 1)).astype(jnp.float32) * (1.0 / period))

    turn = numerator * time
    cos_in = cosine(turn)
    sin_in = cosine(turn + 3 * quarter)
    step = numerator * taps
    cos_step = cosine(step)
    sin_step = cosine(step + 3 * quarter)
    last = turn + numerator * (time_count - taps) + (row & 1) * quarter
    cos_last = cosine(last)
    sin_last = cosine(last + 3 * quarter)
    lag = lax.broadcasted_iota(jnp.int32, (taps, taps), 0)
    late = lax.broadcasted_iota(jnp.int32, (taps, taps), 1)
    kept = jnp.where(lag < taps - late, 1.0, 0.0).astype(jnp.float32)
    fir = fir_ref[...]
    weighted = jnp.concatenate([cos_in * fir, sin_in * fir], 0)
    sums = dot(weighted, kept, precision=lax.Precision.HIGHEST) * (1.0 / math.sqrt(time_count))
    sum_cos = sums[:cols]
    sum_sin = sums[cols:]
    odd = (row & 1) == 1
    cos_own = jnp.where(odd, -sin_in, cos_in)
    sin_own = jnp.where(odd, cos_in, sin_in)
    all_cos = jnp.broadcast_to(sum_cos[:, :1], (cols, taps))
    all_sin = jnp.broadcast_to(sum_sin[:, :1], (cols, taps))
    value = cos_own * all_cos - sin_own * all_sin
    other = sin_own * all_cos + cos_own * all_sin
    tiles = time_count // taps
    for tile in range(tiles):
        if tile == tiles - 1:
            value = cos_last * sum_cos - sin_last * sum_sin
        value_high = value.astype(jnp.bfloat16)
        value_low = (value - value_high.astype(jnp.float32)).astype(jnp.bfloat16)
        table[pl.ds(0, cols), pl.ds(tile * taps, taps)] = value_high
        table[pl.ds(cols, cols), pl.ds(tile * taps, taps)] = value_low
        if tile < tiles - 2:
            value, other = (
                value * cos_step - other * sin_step,
                other * cos_step + value * sin_step,
            )


def fill_sort(sort_ref, rows):
    lines, depth = sort_ref.shape
    half = rows // 2
    line = lax.broadcasted_iota(jnp.int32, (lines, depth), 0)
    place = lax.broadcasted_iota(jnp.int32, (lines, depth), 1)
    group = line // GROUP
    home = (line % GROUP) * rows + (group // 2) % 2 * half + group // 4 * 2 + group % 2
    sort_ref[...] = jnp.where(place == home, 1.0, 0.0).astype(jnp.bfloat16)


def fill_choice(freq_devs, packed, targets_ref, choose, pick, inside, fold, signs):
    count = targets_ref.shape[1]
    shots = choose.shape[1] // 2
    lines, depth = pick.shape
    near_lanes, wide = fold.shape
    near_rows = freq_devs // packed * PARTS
    wanted = jnp.broadcast_to(targets_ref[...].astype(jnp.float32), (128, count)).T
    shot = lax.broadcasted_iota(jnp.int32, (count, 2 * shots), 1) % shots
    choose[...] = jnp.where(shot == wanted[:, :1].astype(jnp.int32), 1.0, 0.0).astype(jnp.bfloat16)

    line = lax.broadcasted_iota(jnp.int32, (lines, depth), 0)
    place = lax.broadcasted_iota(jnp.int32, (lines, depth), 1)
    part = line // shots
    from_shot = line % shots
    from_f = from_shot % freq_devs
    home = (from_shot // freq_devs) * near_rows + (from_f // packed) * PARTS + part
    pick[...] = jnp.where(place == home, 1.0, 0.0).astype(jnp.bfloat16)

    line = lax.broadcasted_iota(jnp.int32, (lines, near_lanes), 0)
    lane = lax.broadcasted_iota(jnp.int32, (lines, near_lanes), 1)
    slot = line % shots % freq_devs % packed
    inside[...] = jnp.where(lane // shots == slot, 1.0, 0.0)

    row = lax.broadcasted_iota(jnp.int32, (near_lanes, wide), 0)
    lane = lax.broadcasted_iota(jnp.int32, (near_lanes, wide), 1)
    spot = lane // (2 * GROUP) * GROUP + lane % GROUP
    fold[...] = jnp.where(row % shots == spot % shots, 1.0, 0.0).astype(jnp.bfloat16)

    source = lax.broadcasted_iota(jnp.int32, (2 * shots, wide), 0) // shots
    lane = lax.broadcasted_iota(jnp.int32, (2 * shots, wide), 1)
    target = lane // GROUP % 2
    used = jnp.where(lane < 2 * shots, 1.0, 0.0)
    signs[0] = jnp.where(source == target, jnp.where(source == 1, -used, used), 0.0)
    signs[1] = jnp.where(source == target, 0.0, used)


def fill_left(plane_ref, choose, pick, inside, fold, signs, left_ref):
    blk_devs, near_rows, near_lanes = plane_ref.shape
    count, depth = choose.shape
    wide = fold.shape[1]
    planes = plane_ref[...].reshape(blk_devs * near_rows, near_lanes)
    near = (dot(pick[...], planes) * inside[...]).astype(jnp.bfloat16)
    near = dot(near, fold[...])
    parts = []
    for i in range(FREQ_DEV):
        for o in range(2):
            parts.append((near[i * depth : (i + 1) * depth] * signs[o]).astype(jnp.bfloat16))
    lefts = dot(choose[...], jnp.concatenate(parts, 1)).astype(jnp.bfloat16)
    for i in range(FREQ_DEV):
        for o in range(2):
            k = 2 * i + o
            left_ref[i, pl.ds(o * count, count), :] = lefts[:, k * wide : (k + 1) * wide]


def product_kernel(recv_ref, left_ref, sort_ref, out_ref, made, sems):
    shots, pieces, rows, lanes = recv_ref.shape
    count = left_ref.shape[1] // 2
    span = GROUP * rows
    scale = 1.0 / math.sqrt(shots)

    def write(i, o):
        return pltpu.make_async_copy(
            made.at[i, pl.ds(o * count, count)], out_ref.at[i, o], sems.at[i, o]
        )

    for i in range(FREQ_DEV):
        lines = sort_ref[pl.ds(i * 4 * GROUP, 4 * GROUP), :]
        rights = []
        for p in range(pieces):
            sorted_rows = []
            for g in range(shots // GROUP):
                received = recv_ref[pl.ds(g * GROUP, GROUP), p].reshape(span, lanes)
                sorted_rows.append(dot(lines, received).astype(jnp.bfloat16))
            for h in range(2):
                part = slice(2 * GROUP * h, 2 * GROUP * (h + 1))
                rights.append(jnp.concatenate([r[part] for r in sorted_rows], 0))
        for o in range(2):
            left = left_ref[i, pl.ds(o * count, count), : 2 * shots]
            for h, right in enumerate(rights):
                made[i, pl.ds(o * count, count), pl.ds(h * lanes, lanes)] = dot(left, right) * scale
            write(i, o).start()

    for i in range(FREQ_DEV):
        for o in range(2):
            write(i, o).wait()


def per_device(traces, fir, targets, band):
    shot_dev, rec_count, time_count = traces.shape
    freq_devs = lax.axis_size("freq")
    blk_devs = lax.axis_size("blk")
    n = freq_devs * blk_devs
    assert shot_dev == 1
    assert blk_devs & (blk_devs - 1) == 0
    col_stride = rec_count // n
    width = rec_count // blk_devs
    lanes = width // 4
    near_lanes = max(128, n)
    packed = near_lanes // n
    near_rows = freq_devs // packed * PARTS
    cols = 2 * FREQ_DEV * freq_devs
    count = targets.shape[0]
    assert n % GROUP == 0
    limit = VMEM_LIMIT if n <= 64 else VMEM_LARGE
    lines = 4 * FREQ_DEV * GROUP
    wide = max(128, 2 * n)
    hbm = lambda x: pltpu.with_memory_space_constraint(x, pltpu.HBM)
    received, lefts, sorter = pl.pallas_call(
        functools.partial(send_kernel, freq_devs, blk_devs, col_stride),
        out_shape=[
            pltpu.VMEM((n, 2, ROWS, lanes), jnp.bfloat16),
            pltpu.VMEM((FREQ_DEV, 2 * count, wide), jnp.bfloat16),
            pltpu.VMEM((lines, GROUP * ROWS), jnp.bfloat16),
        ],
        in_specs=[pl.BlockSpec(memory_space=pl.ANY)] * 4,
        out_specs=[pl.BlockSpec(memory_space=pltpu.VMEM)] * 3,
        scratch_shapes=[
            pltpu.SMEM((2,), jnp.int32),
            pltpu.VMEM((1, fir.shape[0]), jnp.float32),
            pltpu.VMEM((1, count), jnp.int32),
            pltpu.VMEM((n, col_stride, time_count), jnp.bfloat16),
            pltpu.VMEM((n, 16, time_count), jnp.bfloat16),
            pltpu.VMEM((2 * cols, time_count), jnp.bfloat16),
            pltpu.VMEM((blk_devs, freq_devs, 2, ROWS, lanes), jnp.bfloat16),
            pltpu.VMEM((freq_devs, near_rows, near_lanes), jnp.bfloat16),
            pltpu.VMEM((freq_devs, near_rows, near_lanes), jnp.bfloat16),
            pltpu.VMEM((near_rows, near_lanes), jnp.bfloat16),
            pltpu.VMEM((blk_devs, near_rows, near_lanes), jnp.bfloat16),
            pltpu.VMEM((count, 2 * n), jnp.bfloat16),
            pltpu.VMEM((FREQ_DEV * 2 * n, blk_devs * near_rows), jnp.bfloat16),
            pltpu.VMEM((FREQ_DEV * 2 * n, near_lanes), jnp.float32),
            pltpu.VMEM((near_lanes, wide), jnp.bfloat16),
            pltpu.VMEM((2, 2 * n, wide), jnp.float32),
            pltpu.SemaphoreType.DMA((3,)),
            pltpu.SemaphoreType.DMA((blk_devs, 2)),
            pltpu.SemaphoreType.DMA,
            pltpu.SemaphoreType.DMA((blk_devs,)),
            pltpu.SemaphoreType.DMA,
            pltpu.SemaphoreType.DMA,
            pltpu.SemaphoreType.DMA,
            pltpu.SemaphoreType.DMA,
            pltpu.SemaphoreType.DMA,
        ],
        compiler_params=pltpu.CompilerParams(
            collective_id=0, has_side_effects=True, vmem_limit_bytes=limit
        ),
    )(
        hbm(band),
        hbm(fir.reshape(1, -1)),
        hbm(targets.reshape(1, -1)),
        hbm(traces.reshape(n, col_stride, time_count)),
    )
    return pl.pallas_call(
        product_kernel,
        out_shape=jax.ShapeDtypeStruct((FREQ_DEV, 2, count, width), jnp.float32),
        in_specs=[pl.BlockSpec(memory_space=pltpu.VMEM)] * 3,
        out_specs=pl.BlockSpec(memory_space=pl.ANY),
        scratch_shapes=[
            pltpu.VMEM((FREQ_DEV, 2 * count, width), jnp.float32),
            pltpu.SemaphoreType.DMA((FREQ_DEV, 2)),
        ],
        compiler_params=pltpu.CompilerParams(vmem_limit_bytes=limit),
    )(received, lefts, sorter)


def solution(mesh):
    placed = (P(("blk", "freq"), None, None), P(), P(), P())
    return jax.shard_map(
        per_device,
        mesh=mesh,
        in_specs=placed,
        out_specs=P("freq", None, None, "blk"),
        check_vma=False,
    )
```

```python
import functools
import math

import jax
import jax.numpy as jnp
from jax import lax
from jax.experimental import pallas as pl
from jax.experimental.pallas import tpu as pltpu
from jax.sharding import PartitionSpec as P

FREQ_DEV = 4
PARTS = 2 * FREQ_DEV
ROWS = 2 * PARTS
VMEM_LIMIT = 40 * 2**20
VMEM_LARGE = 58 * 2**20
GROUP = 32
UNROLL = True
MESH = pl.DeviceIdType.MESH


def dot(a, b, dims=(((1,), (0,)), ((), ())), precision=None):
    return lax.dot_general(a, b, dims, precision=precision, preferred_element_type=jnp.float32)


def cos_turns(turns):
    w = (0.25 - jnp.abs(turns - 0.5)) * (2.0 * math.pi)
    w2 = w * w
    total = jnp.full_like(w, 1.0 / math.factorial(13))
    for order in (11, 9, 7, 5, 3, 1):
        sign = 1.0 if order % 4 == 1 else -1.0
        total = total * w2 + sign / math.factorial(order)
    return -(total * w)


def flipped(index, offset, count):
    total = 0
    bit = 1
    while bit < count:
        total = total + bit * lax.rem(index // bit + (offset // bit) % 2, 2)
        bit *= 2
    return total


def send_kernel(
    freq_devs, blk_devs, col_stride,
    band_hbm, fir_hbm, targets_hbm, traces_ref, recv_ref, left_ref, sort_ref,
    band_ref, fir_ref, targets_ref,
    traces_buf, spots_buf, table, outgoing, relay, near_out, near_in, plane_out, plane_ref,
    choose, pick, inside, fold, signs,
    small_sem, chunk_sem, spot_sem, send_sem, recv_sem,
    near_send, near_recv, plane_send, plane_recv, relay_send, relay_recv, go,
):
    me_f = lax.axis_index("freq")
    me_b = lax.axis_index("blk")
    me = me_b * freq_devs + me_f
    n = freq_devs * blk_devs
    spots, _, time_count = traces_buf.shape
    rec_count = spots * col_stride
    width = rec_count // blk_devs
    lanes = width // 4
    freq_count = FREQ_DEV * freq_devs
    cols = 2 * freq_count
    per = width // col_stride
    _, near_rows, near_lanes = near_out.shape
    packed = near_lanes // spots

    side = blk_devs // 2
    high = me_b // side
    depth = (1 - high) * (side - 1 - me_b) + high * (me_b - side)
    mate_b = blk_devs - 1 - me_b
    mate = mate_b * freq_devs + me_f
    inner = depth == 0
    last = me_b == blk_devs - 1
    ranks = [lax.rem(depth + step, side) for step in range(side)]
    blocks = [(1 - high) * (side + r) + high * (side - 1 - r) for r in ranks]
    blocks += [high * side + lax.rem(me_b + 1 + step, side) for step in range(side)]
    late = (me_b // side)
    delayed = blocks[1]
    blocks[1] = (1 - late) * delayed + late * blocks[side]
    blocks[side] = (1 - late) * blocks[side] + late * delayed
    piece = per // 2

    def spot_copy():
        return pltpu.make_async_copy(
            traces_ref.at[:, pl.ds(0, 16), :], spots_buf, spot_sem
        )

    def chunk_copy(step, part):
        return pltpu.make_async_copy(
            traces_ref.at[pl.ds(blocks[step] * per + part * piece, piece)],
            traces_buf.at[pl.ds(step * per + part * piece, piece)],
            chunk_sem.at[step, part],
        )

    def signal(f, block, sem):
        pl.semaphore_signal(sem, inc=1, device_id=(f, block), device_id_type=MESH)

    def signal_block(block, first):
        @pl.loop(first, freq_devs, unroll=UNROLL)
        def _(d):
            signal(lax.rem(me_f + d, freq_devs), block, barrier)

    def announce():
        @pl.when(inner)
        def _():
            signal(me_f, mate_b, barrier)

        for block in range(blk_devs - 1, -1, -1):
            if block not in (side - 1, side):

                @pl.when(me_b == block)
                def _():
                    signal_block(block, 1)

                @pl.when(me_b != block)
                def _():
                    signal_block(block, 0)

    def near_copy(f):
        return pltpu.make_async_remote_copy(
            src_ref=near_out.at[f],
            dst_ref=near_in.at[me_f],
            send_sem=near_send,
            recv_sem=near_recv,
            device_id=(f, me_b),
            device_id_type=MESH,
        )

    def plane_copy(offset, slot):
        return pltpu.make_async_remote_copy(
            src_ref=plane_out,
            dst_ref=plane_ref.at[slot],
            send_sem=plane_send,
            recv_sem=plane_recv,
            device_id=(me_f, flipped(me_b, offset, blk_devs)),
            device_id_type=MESH,
        )

    def send(step, parts):
        first = 1 if step == blk_devs - 1 else 0
        turn = me_f if first else me_f * jnp.minimum(blocks[step], 1)

        @pl.loop(first, freq_devs, unroll=UNROLL)
        def _(d):
            f = lax.rem(turn + d, freq_devs)
            pltpu.make_async_remote_copy(
                src_ref=outgoing.at[step, f, parts],
                dst_ref=recv_ref.at[me, parts],
                send_sem=send_sem.at[step],
                recv_sem=recv_sem,
                device_id=(f, blocks[step]),
                device_id_type=MESH,
            ).start()

    def relay_copy(part):
        return pltpu.make_async_remote_copy(
            src_ref=outgoing.at[0, :, pl.ds(part, 1)],
            dst_ref=relay.at[:, pl.ds(part, 1)],
            send_sem=send_sem.at[0],
            recv_sem=relay_recv.at[part],
            device_id=(me_f, mate_b),
            device_id_type=MESH,
        )

    def forward():
        for part in range(2):
            relay_copy(part).wait_recv()
        recv_ref[mate] = relay[me_f]

        @pl.loop(1, freq_devs, unroll=UNROLL)
        def _(d):
            f = lax.rem(me_f + d, freq_devs)
            pltpu.make_async_remote_copy(
                src_ref=relay.at[f],
                dst_ref=recv_ref.at[mate],
                send_sem=relay_send,
                recv_sem=recv_sem,
                device_id=(f, me_b),
                device_id_type=MESH,
            ).start()

    def arrived(ref, sem):
        pltpu.make_async_copy(ref, ref, sem).wait()

    small = [
        pltpu.make_async_copy(band_hbm, band_ref, small_sem.at[0]),
        pltpu.make_async_copy(fir_hbm, fir_ref, small_sem.at[1]),
        pltpu.make_async_copy(targets_hbm, targets_ref, small_sem.at[2]),
    ]
    barrier = pltpu.get_barrier_semaphore()
    small[0].start()
    small[1].start()
    chunk_copy(0, 0).start()
    with jax.named_scope("signals"):
        announce()
    spot_copy().start()
    with jax.named_scope("small_wait"):
        small[0].wait()
        small[1].wait()
    chunk_copy(0, 1).start()
    with jax.named_scope("table"):
        fill_table(band_ref, fir_ref, table, freq_count)

    def spectrum_of(rows):
        both = dot(table[...], rows, (((1,), (1,)), ((), ())))
        return both[:cols] + both[cols:]

    def spectra(step, part):
        with jax.named_scope(f"chunk{step}{part}"):
            chunk_copy(step, part).wait()
            rows = traces_buf[pl.ds(step * per + part * piece, piece)]
            values = spectrum_of(rows.reshape(2 * lanes, time_count))
            values = values.reshape(freq_devs, PARTS, 2 * lanes)
            values = jnp.concatenate([values[:, :, :lanes], values[:, :, lanes:]], 1)
            outgoing[step, :, part] = values.astype(jnp.bfloat16)

    chunk_copy(1, 0).start()
    small[2].start()
    @pl.when(last)
    def _():
        with jax.named_scope("barrier"):
            pl.semaphore_wait(barrier, n - 1)
        signal(me_f, side, go)
        signal(me_f, side - 1, go)

    for part in range(2):
        spectra(0, part)

        @pl.when(inner)
        def _():
            if part == 0:
                with jax.named_scope("mate"):
                    pl.semaphore_wait(barrier, 1)
            relay_copy(part).start()

        @pl.when(last)
        def _():
            send(0, pl.ds(part, 1))

        if part == 0:
            chunk_copy(1, 1).start()
            for step in range(2, blk_devs):
                chunk_copy(step, 0).start()
                chunk_copy(step, 1).start()

    with jax.named_scope("spots"):
        spot_copy().wait()
        near = spectrum_of(spots_buf[...].reshape(spots * 16, time_count)).astype(jnp.bfloat16)
        spot_row = lax.broadcasted_iota(jnp.int32, (spots * 16, near_lanes), 0)
        spot_col = lax.broadcasted_iota(jnp.int32, (spots * 16, near_lanes), 1)
        shift = lax.rem(me_f, packed) * spots
        at_spot = jnp.where(spot_row == (spot_col - shift) * 16, 1.0, 0.0).astype(jnp.bfloat16)
        at_spots = dot(near, at_spot).reshape(freq_devs, PARTS, near_lanes)
        at_spots = jnp.concatenate([at_spots] * (near_rows // PARTS), 1)
        line = lax.broadcasted_iota(jnp.int32, at_spots.shape, 1) // PARTS
        near_out[...] = jnp.where(line == me_f // packed, at_spots, 0.0).astype(jnp.bfloat16)
        near_in[me_f] = near_out[me_f]

    @pl.when(inner)
    def _():
        with jax.named_scope("go"):
            pl.semaphore_wait(go, 1)

    outer_rest = jnp.logical_not(jnp.logical_or(inner, last))

    @pl.when(outer_rest)
    def _():
        with jax.named_scope("barrier"):
            pl.semaphore_wait(barrier, n - 1)

    @pl.loop(1, freq_devs, unroll=UNROLL)
    def _(d):
        near_copy(lax.rem(me_f + d, freq_devs)).start()

    @pl.when(outer_rest)
    def _():
        send(0, pl.ds(0, 2))

    spectra(1, 0)
    send(1, pl.ds(0, 1))
    spectra(1, 1)
    spectra(2, 0)
    spectra(2, 1)
    with jax.named_scope("plane"):
        arrived(near_in.at[pl.ds(0, freq_devs - 1)], near_recv)
        total = near_in[...].astype(jnp.float32)
        plane_out[...] = jnp.sum(total, 0).astype(jnp.bfloat16)
        plane_ref[me_b] = plane_out[...]
    for offset in range(1, blk_devs):
        plane_copy(offset, me_b).start()
    send(1, pl.ds(1, 1))
    send(2, pl.ds(0, 2))
    for step in range(3, blk_devs):
        spectra(step, 0)
        spectra(step, 1)
        if step == blk_devs - 1:
            recv_ref[me] = outgoing[step, me_f]
        send(step, pl.ds(0, 2))

    with jax.named_scope("sort"):
        fill_sort(sort_ref, recv_ref.shape[2])
    with jax.named_scope("choice"):
        small[2].wait()
        fill_choice(freq_devs, packed, targets_ref, choose, pick, inside, fold, signs)

    @pl.when(inner)
    def _():
        with jax.named_scope("forward"):
            forward()

    with jax.named_scope("plane_wait"):
        arrived(plane_ref.at[pl.ds(0, blk_devs - 1)], plane_recv)
    with jax.named_scope("left"):
        fill_left(plane_ref, choose, pick, inside, fold, signs, left_ref)
    with jax.named_scope("send_wait"):
        arrived(near_in.at[pl.ds(0, freq_devs - 1)], near_send)
        arrived(plane_ref.at[pl.ds(0, blk_devs - 1)], plane_send)
        for step in range(blk_devs - 1):
            arrived(outgoing.at[step], send_sem.at[step])
        arrived(outgoing.at[blk_devs - 1, pl.ds(0, freq_devs - 1)], send_sem.at[blk_devs - 1])
    with jax.named_scope("recv_wait"):

        @pl.when(inner)
        def _():
            arrived(relay.at[pl.ds(0, freq_devs - 1)], relay_send)
            arrived(recv_ref.at[pl.ds(0, n - 2)], recv_sem)

        @pl.when(jnp.logical_not(inner))
        def _():
            arrived(recv_ref.at[pl.ds(0, n - 1)], recv_sem)


def fill_table(band_ref, fir_ref, table, freq_count):
    cols = table.shape[0] // 2
    time_count = table.shape[1]
    taps = fir_ref.shape[1]
    period = freq_count * time_count
    quarter = period // 4
    row = lax.broadcasted_iota(jnp.int32, (cols, taps), 0)
    time = lax.broadcasted_iota(jnp.int32, (cols, taps), 1)
    low = band_ref[0]
    high = band_ref[1]
    numerator = low * freq_count + (high - low) * (row >> 1)

    def cosine(turn):
        return cos_turns((turn & (period - 1)).astype(jnp.float32) * (1.0 / period))

    turn = numerator * time
    cos_in = cosine(turn)
    sin_in = cosine(turn + 3 * quarter)
    step = numerator * taps
    cos_step = cosine(step)
    sin_step = cosine(step + 3 * quarter)
    last = turn + numerator * (time_count - taps) + (row & 1) * quarter
    cos_last = cosine(last)
    sin_last = cosine(last + 3 * quarter)
    lag = lax.broadcasted_iota(jnp.int32, (taps, taps), 0)
    late = lax.broadcasted_iota(jnp.int32, (taps, taps), 1)
    kept = jnp.where(lag < taps - late, 1.0, 0.0).astype(jnp.float32)
    fir = fir_ref[...]
    weighted = jnp.concatenate([cos_in * fir, sin_in * fir], 0)
    sums = dot(weighted, kept, precision=lax.Precision.HIGHEST) * (1.0 / math.sqrt(time_count))
    sum_cos = sums[:cols]
    sum_sin = sums[cols:]
    odd = (row & 1) == 1
    cos_own = jnp.where(odd, -sin_in, cos_in)
    sin_own = jnp.where(odd, cos_in, sin_in)
    all_cos = jnp.broadcast_to(sum_cos[:, :1], (cols, taps))
    all_sin = jnp.broadcast_to(sum_sin[:, :1], (cols, taps))
    value = cos_own * all_cos - sin_own * all_sin
    other = sin_own * all_cos + cos_own * all_sin
    tiles = time_count // taps
    for tile in range(tiles):
        if tile == tiles - 1:
            value = cos_last * sum_cos - sin_last * sum_sin
        value_high = value.astype(jnp.bfloat16)
        value_low = (value - value_high.astype(jnp.float32)).astype(jnp.bfloat16)
        table[pl.ds(0, cols), pl.ds(tile * taps, taps)] = value_high
        table[pl.ds(cols, cols), pl.ds(tile * taps, taps)] = value_low
        if tile < tiles - 2:
            value, other = (
                value * cos_step - other * sin_step,
                other * cos_step + value * sin_step,
            )


def fill_sort(sort_ref, rows):
    lines, depth = sort_ref.shape
    half = rows // 2
    line = lax.broadcasted_iota(jnp.int32, (lines, depth), 0)
    place = lax.broadcasted_iota(jnp.int32, (lines, depth), 1)
    group = line // GROUP
    home = (line % GROUP) * rows + (group // 2) % 2 * half + group // 4 * 2 + group % 2
    sort_ref[...] = jnp.where(place == home, 1.0, 0.0).astype(jnp.bfloat16)


def fill_choice(freq_devs, packed, targets_ref, choose, pick, inside, fold, signs):
    count = targets_ref.shape[1]
    shots = choose.shape[1] // 2
    lines, depth = pick.shape
    near_lanes, wide = fold.shape
    near_rows = freq_devs // packed * PARTS
    wanted = jnp.broadcast_to(targets_ref[...].astype(jnp.float32), (128, count)).T
    shot = lax.broadcasted_iota(jnp.int32, (count, 2 * shots), 1) % shots
    choose[...] = jnp.where(shot == wanted[:, :1].astype(jnp.int32), 1.0, 0.0).astype(jnp.bfloat16)

    line = lax.broadcasted_iota(jnp.int32, (lines, depth), 0)
    place = lax.broadcasted_iota(jnp.int32, (lines, depth), 1)
    part = line // shots
    from_shot = line % shots
    from_f = from_shot % freq_devs
    home = (from_shot // freq_devs) * near_rows + (from_f // packed) * PARTS + part
    pick[...] = jnp.where(place == home, 1.0, 0.0).astype(jnp.bfloat16)

    line = lax.broadcasted_iota(jnp.int32, (lines, near_lanes), 0)
    lane = lax.broadcasted_iota(jnp.int32, (lines, near_lanes), 1)
    slot = line % shots % freq_devs % packed
    inside[...] = jnp.where(lane // shots == slot, 1.0, 0.0)

    row = lax.broadcasted_iota(jnp.int32, (near_lanes, wide), 0)
    lane = lax.broadcasted_iota(jnp.int32, (near_lanes, wide), 1)
    spot = lane // (2 * GROUP) * GROUP + lane % GROUP
    fold[...] = jnp.where(row % shots == spot % shots, 1.0, 0.0).astype(jnp.bfloat16)

    source = lax.broadcasted_iota(jnp.int32, (2 * shots, wide), 0) // shots
    lane = lax.broadcasted_iota(jnp.int32, (2 * shots, wide), 1)
    target = lane // GROUP % 2
    used = jnp.where(lane < 2 * shots, 1.0, 0.0)
    signs[0] = jnp.where(source == target, jnp.where(source == 1, -used, used), 0.0)
    signs[1] = jnp.where(source == target, 0.0, used)


def fill_left(plane_ref, choose, pick, inside, fold, signs, left_ref):
    blk_devs, near_rows, near_lanes = plane_ref.shape
    count, depth = choose.shape
    wide = fold.shape[1]
    planes = plane_ref[...].reshape(blk_devs * near_rows, near_lanes)
    near = (dot(pick[...], planes) * inside[...]).astype(jnp.bfloat16)
    near = dot(near, fold[...])
    parts = []
    for i in range(FREQ_DEV):
        for o in range(2):
            parts.append((near[i * depth : (i + 1) * depth] * signs[o]).astype(jnp.bfloat16))
    lefts = dot(choose[...], jnp.concatenate(parts, 1)).astype(jnp.bfloat16)
    for i in range(FREQ_DEV):
        for o in range(2):
            k = 2 * i + o
            left_ref[i, pl.ds(o * count, count), :] = lefts[:, k * wide : (k + 1) * wide]


def product_kernel(recv_ref, left_ref, sort_ref, out_ref, made, sems):
    shots, pieces, rows, lanes = recv_ref.shape
    count = left_ref.shape[1] // 2
    span = GROUP * rows
    scale = 1.0 / math.sqrt(shots)

    def write(i, o):
        return pltpu.make_async_copy(
            made.at[i, pl.ds(o * count, count)], out_ref.at[i, o], sems.at[i, o]
        )

    for i in range(FREQ_DEV):
        lines = sort_ref[pl.ds(i * 4 * GROUP, 4 * GROUP), :]
        rights = []
        for p in range(pieces):
            sorted_rows = []
            for g in range(shots // GROUP):
                received = recv_ref[pl.ds(g * GROUP, GROUP), p].reshape(span, lanes)
                sorted_rows.append(dot(lines, received).astype(jnp.bfloat16))
            for h in range(2):
                part = slice(2 * GROUP * h, 2 * GROUP * (h + 1))
                rights.append(jnp.concatenate([r[part] for r in sorted_rows], 0))
        for o in range(2):
            left = left_ref[i, pl.ds(o * count, count), : 2 * shots]
            for h, right in enumerate(rights):
                made[i, pl.ds(o * count, count), pl.ds(h * lanes, lanes)] = dot(left, right) * scale
            write(i, o).start()

    for i in range(FREQ_DEV):
        for o in range(2):
            write(i, o).wait()


def per_device(traces, fir, targets, band):
    shot_dev, rec_count, time_count = traces.shape
    freq_devs = lax.axis_size("freq")
    blk_devs = lax.axis_size("blk")
    n = freq_devs * blk_devs
    assert shot_dev == 1
    assert blk_devs & (blk_devs - 1) == 0
    col_stride = rec_count // n
    width = rec_count // blk_devs
    lanes = width // 4
    near_lanes = max(128, n)
    packed = near_lanes // n
    near_rows = freq_devs // packed * PARTS
    cols = 2 * FREQ_DEV * freq_devs
    count = targets.shape[0]
    assert n % GROUP == 0
    limit = VMEM_LIMIT if n <= 64 else VMEM_LARGE
    lines = 4 * FREQ_DEV * GROUP
    wide = max(128, 2 * n)
    hbm = lambda x: pltpu.with_memory_space_constraint(x, pltpu.HBM)
    received, lefts, sorter = pl.pallas_call(
        functools.partial(send_kernel, freq_devs, blk_devs, col_stride),
        out_shape=[
            pltpu.VMEM((n, 2, ROWS, lanes), jnp.bfloat16),
            pltpu.VMEM((FREQ_DEV, 2 * count, wide), jnp.bfloat16),
            pltpu.VMEM((lines, GROUP * ROWS), jnp.bfloat16),
        ],
        in_specs=[pl.BlockSpec(memory_space=pl.ANY)] * 4,
        out_specs=[pl.BlockSpec(memory_space=pltpu.VMEM)] * 3,
        scratch_shapes=[
            pltpu.SMEM((2,), jnp.int32),
            pltpu.VMEM((1, fir.shape[0]), jnp.float32),
            pltpu.VMEM((1, count), jnp.int32),
            pltpu.VMEM((n, col_stride, time_count), jnp.bfloat16),
            pltpu.VMEM((n, 16, time_count), jnp.bfloat16),
            pltpu.VMEM((2 * cols, time_count), jnp.bfloat16),
            pltpu.VMEM((blk_devs, freq_devs, 2, ROWS, lanes), jnp.bfloat16),
            pltpu.VMEM((freq_devs, 2, ROWS, lanes), jnp.bfloat16),
            pltpu.VMEM((freq_devs, near_rows, near_lanes), jnp.bfloat16),
            pltpu.VMEM((freq_devs, near_rows, near_lanes), jnp.bfloat16),
            pltpu.VMEM((near_rows, near_lanes), jnp.bfloat16),
            pltpu.VMEM((blk_devs, near_rows, near_lanes), jnp.bfloat16),
            pltpu.VMEM((count, 2 * n), jnp.bfloat16),
            pltpu.VMEM((FREQ_DEV * 2 * n, blk_devs * near_rows), jnp.bfloat16),
            pltpu.VMEM((FREQ_DEV * 2 * n, near_lanes), jnp.float32),
            pltpu.VMEM((near_lanes, wide), jnp.bfloat16),
            pltpu.VMEM((2, 2 * n, wide), jnp.float32),
            pltpu.SemaphoreType.DMA((3,)),
            pltpu.SemaphoreType.DMA((blk_devs, 2)),
            pltpu.SemaphoreType.DMA,
            pltpu.SemaphoreType.DMA((blk_devs,)),
            pltpu.SemaphoreType.DMA,
            pltpu.SemaphoreType.DMA,
            pltpu.SemaphoreType.DMA,
            pltpu.SemaphoreType.DMA,
            pltpu.SemaphoreType.DMA,
            pltpu.SemaphoreType.DMA,
            pltpu.SemaphoreType.DMA((2,)),
            pltpu.SemaphoreType.REGULAR,
        ],
        compiler_params=pltpu.CompilerParams(
            collective_id=0, has_side_effects=True, vmem_limit_bytes=limit
        ),
    )(
        hbm(band),
        hbm(fir.reshape(1, -1)),
        hbm(targets.reshape(1, -1)),
        hbm(traces.reshape(n, col_stride, time_count)),
    )
    return pl.pallas_call(
        product_kernel,
        out_shape=jax.ShapeDtypeStruct((FREQ_DEV, 2, count, width), jnp.float32),
        in_specs=[pl.BlockSpec(memory_space=pltpu.VMEM)] * 3,
        out_specs=pl.BlockSpec(memory_space=pl.ANY),
        scratch_shapes=[
            pltpu.VMEM((FREQ_DEV, 2 * count, width), jnp.float32),
            pltpu.SemaphoreType.DMA((FREQ_DEV, 2)),
        ],
        compiler_params=pltpu.CompilerParams(vmem_limit_bytes=limit),
    )(received, lefts, sorter)


def solution(mesh):
    placed = (P(("blk", "freq"), None, None), P(), P(), P())
    return jax.shard_map(
        per_device,
        mesh=mesh,
        in_specs=placed,
        out_specs=P("freq", None, None, "blk"),
        check_vma=False,
    )
```

```python
import functools
import math

import jax
import jax.numpy as jnp
from jax import lax
from jax.experimental import pallas as pl
from jax.experimental.pallas import tpu as pltpu
from jax.sharding import PartitionSpec as P

FREQ_DEV = 4
PARTS = 2 * FREQ_DEV
ROWS = 2 * PARTS
VMEM_LIMIT = 40 * 2**20
VMEM_LARGE = 52 * 2**20
GROUP = 32
UNROLL = True
MESH = pl.DeviceIdType.MESH


def dot(a, b, dims=(((1,), (0,)), ((), ())), precision=None):
    return lax.dot_general(a, b, dims, precision=precision, preferred_element_type=jnp.float32)


def cos_turns(turns):
    w = (0.25 - jnp.abs(turns - 0.5)) * (2.0 * math.pi)
    w2 = w * w
    total = jnp.full_like(w, 1.0 / math.factorial(13))
    for order in (11, 9, 7, 5, 3, 1):
        sign = 1.0 if order % 4 == 1 else -1.0
        total = total * w2 + sign / math.factorial(order)
    return -(total * w)


def flipped(index, offset, count):
    total = 0
    bit = 1
    while bit < count:
        total = total + bit * lax.rem(index // bit + (offset // bit) % 2, 2)
        bit *= 2
    return total


def send_kernel(
    freq_devs, blk_devs, col_stride,
    band_hbm, fir_hbm, targets_hbm, traces_ref, recv_ref, left_ref, sort_ref, early_ref,
    band_ref, fir_ref, targets_ref,
    traces_buf, spots_buf, table, outgoing, relay, near_out, near_in, plane_out, plane_ref,
    choose, pick, inside, fold, signs,
    small_sem, chunk_sem, spot_sem, send_sem, recv_sem,
    near_send, near_recv, plane_send, plane_recv, relay_send, relay_recv, go,
):
    me_f = lax.axis_index("freq")
    me_b = lax.axis_index("blk")
    me = me_b * freq_devs + me_f
    n = freq_devs * blk_devs
    spots, _, time_count = traces_buf.shape
    rec_count = spots * col_stride
    width = rec_count // blk_devs
    lanes = width // 4
    freq_count = FREQ_DEV * freq_devs
    cols = 2 * freq_count
    per = width // col_stride
    _, near_rows, near_lanes = near_out.shape
    packed = near_lanes // spots

    side = blk_devs // 2
    high = me_b // side
    depth = (1 - high) * (side - 1 - me_b) + high * (me_b - side)
    mate_b = blk_devs - 1 - me_b
    mate = mate_b * freq_devs + me_f
    inner = depth == 0
    last = me_b == blk_devs - 1
    ranks = [lax.rem(depth + step, side) for step in range(side)]
    blocks = [(1 - high) * (side + r) + high * (side - 1 - r) for r in ranks]
    blocks += [high * side + lax.rem(me_b + 1 + step, side) for step in range(side)]
    late = (me_b // side)
    delayed = blocks[1]
    blocks[1] = (1 - late) * delayed + late * blocks[side]
    blocks[side] = (1 - late) * blocks[side] + late * delayed
    piece = per // 2

    def spot_copy():
        return pltpu.make_async_copy(
            traces_ref.at[:, pl.ds(0, 16), :], spots_buf, spot_sem
        )

    def chunk_copy(step, part):
        return pltpu.make_async_copy(
            traces_ref.at[pl.ds(blocks[step] * per + part * piece, piece)],
            traces_buf.at[pl.ds(step * per + part * piece, piece)],
            chunk_sem.at[step, part],
        )

    def signal(f, block, sem):
        pl.semaphore_signal(sem, inc=1, device_id=(f, block), device_id_type=MESH)

    def signal_block(block, first):
        @pl.loop(first, freq_devs, unroll=UNROLL)
        def _(d):
            signal(lax.rem(me_f + d, freq_devs), block, barrier)

    def announce():
        @pl.when(inner)
        def _():
            signal(me_f, mate_b, barrier)

        for block in range(blk_devs - 1, -1, -1):
            if block not in (side - 1, side):

                @pl.when(me_b == block)
                def _():
                    signal_block(block, 1)

                @pl.when(me_b != block)
                def _():
                    signal_block(block, 0)

    def near_copy(f):
        return pltpu.make_async_remote_copy(
            src_ref=near_out.at[f],
            dst_ref=near_in.at[me_f],
            send_sem=near_send,
            recv_sem=near_recv,
            device_id=(f, me_b),
            device_id_type=MESH,
        )

    def plane_copy(offset, slot):
        return pltpu.make_async_remote_copy(
            src_ref=plane_out,
            dst_ref=plane_ref.at[slot],
            send_sem=plane_send,
            recv_sem=plane_recv,
            device_id=(me_f, flipped(me_b, offset, blk_devs)),
            device_id_type=MESH,
        )

    def send(step, part, some=None):
        first = 1 if step == blk_devs - 1 else 0
        turn = me_f if first else me_f * jnp.minimum(blocks[step], 1)

        start, stop = some or (first, freq_devs)

        @pl.loop(start, stop, unroll=UNROLL)
        def _(d):
            f = lax.rem(turn + d, freq_devs)
            pltpu.make_async_remote_copy(
                src_ref=outgoing.at[step, f, part],
                dst_ref=recv_ref.at[me, part],
                send_sem=send_sem.at[step],
                recv_sem=recv_sem.at[part],
                device_id=(f, blocks[step]),
                device_id_type=MESH,
            ).start()

    def relay_copy(part):
        return pltpu.make_async_remote_copy(
            src_ref=outgoing.at[0, :, pl.ds(part, 1)],
            dst_ref=relay.at[:, pl.ds(part, 1)],
            send_sem=send_sem.at[0],
            recv_sem=relay_recv.at[part],
            device_id=(me_f, mate_b),
            device_id_type=MESH,
        )

    def forward(part):
        relay_copy(part).wait_recv()
        recv_ref[mate, part] = relay[me_f, part]

        @pl.loop(1, freq_devs, unroll=UNROLL)
        def _(d):
            f = lax.rem(me_f + d, freq_devs)
            pltpu.make_async_remote_copy(
                src_ref=relay.at[f, part],
                dst_ref=recv_ref.at[mate, part],
                send_sem=relay_send,
                recv_sem=recv_sem.at[part],
                device_id=(f, me_b),
                device_id_type=MESH,
            ).start()

    def wait_part(part):
        @pl.when(inner)
        def _():
            arrived(recv_ref.at[pl.ds(0, n - 2), part], recv_sem.at[part])

        @pl.when(jnp.logical_not(inner))
        def _():
            arrived(recv_ref.at[pl.ds(0, n - 1), part], recv_sem.at[part])

    def arrived(ref, sem):
        pltpu.make_async_copy(ref, ref, sem).wait()

    small = [
        pltpu.make_async_copy(band_hbm, band_ref, small_sem.at[0]),
        pltpu.make_async_copy(fir_hbm, fir_ref, small_sem.at[1]),
        pltpu.make_async_copy(targets_hbm, targets_ref, small_sem.at[2]),
    ]
    barrier = pltpu.get_barrier_semaphore()
    small[0].start()
    small[1].start()
    chunk_copy(0, 0).start()
    with jax.named_scope("signals"):
        announce()
    spot_copy().start()
    with jax.named_scope("small_wait"):
        small[0].wait()
        small[1].wait()
    chunk_copy(0, 1).start()
    with jax.named_scope("table"):
        fill_table(band_ref, fir_ref, table, freq_count)

    def spectrum_of(rows):
        both = dot(table[...], rows, (((1,), (1,)), ((), ())))
        return both[:cols] + both[cols:]

    def spectra(step, part):
        with jax.named_scope(f"chunk{step}{part}"):
            chunk_copy(step, part).wait()
            rows = traces_buf[pl.ds(step * per + part * piece, piece)]
            values = spectrum_of(rows.reshape(2 * lanes, time_count))
            values = values.reshape(freq_devs, PARTS, 2 * lanes)
            values = jnp.concatenate([values[:, :, :lanes], values[:, :, lanes:]], 1)
            outgoing[step, :, part] = values.astype(jnp.bfloat16)

    chunk_copy(1, 0).start()
    small[2].start()
    def spots_near():
        with jax.named_scope("spots"):
            spot_copy().wait()
            shift = lax.rem(me_f, packed) * spots
            taken = min(spots, 64)
            at_spots = None
            for first in range(0, spots, taken):
                rows = spots_buf[pl.ds(first, taken)].reshape(taken * 16, time_count)
                near = spectrum_of(rows).astype(jnp.bfloat16)
                spot_row = lax.broadcasted_iota(jnp.int32, (taken * 16, near_lanes), 0)
                spot_col = lax.broadcasted_iota(jnp.int32, (taken * 16, near_lanes), 1)
                here = spot_row == (spot_col - shift - first) * 16
                some = dot(near, jnp.where(here, 1.0, 0.0).astype(jnp.bfloat16))
                at_spots = some if at_spots is None else at_spots + some
            at_spots = at_spots.reshape(freq_devs, PARTS, near_lanes)
            at_spots = jnp.concatenate([at_spots] * 2, 1)
            line = lax.broadcasted_iota(jnp.int32, at_spots.shape, 1) // PARTS
            for pair in range(near_rows // (2 * PARTS)):
                kept = jnp.where(line + 2 * pair == me_f // packed, at_spots, 0.0)
                near_out[:, pl.ds(2 * PARTS * pair, 2 * PARTS), :] = kept.astype(jnp.bfloat16)
            near_in[me_f] = near_out[me_f]

    def send_near():

        @pl.loop(1, freq_devs, unroll=UNROLL)
        def _(d):
            near_copy(lax.rem(me_f + d, freq_devs)).start()

    @pl.when(last)
    def _():
        with jax.named_scope("barrier"):
            pl.semaphore_wait(barrier, n - 1)
        signal(me_f, side, go)
        signal(me_f, side - 1, go)
        spots_near()
        send_near()

    for part in range(2):
        spectra(0, part)

        @pl.when(inner)
        def _():
            if part == 0:
                with jax.named_scope("mate"):
                    pl.semaphore_wait(barrier, 1)
            relay_copy(part).start()

        @pl.when(last)
        def _():
            send(0, part)

        if part == 0:
            chunk_copy(1, 1).start()
            for step in range(2, blk_devs):
                chunk_copy(step, 0).start()
                chunk_copy(step, 1).start()

    outer_rest = jnp.logical_not(jnp.logical_or(inner, last))

    @pl.when(jnp.logical_not(last))
    def _():
        spots_near()

    @pl.when(inner)
    def _():
        with jax.named_scope("go"):
            pl.semaphore_wait(go, 1)

    @pl.when(outer_rest)
    def _():
        with jax.named_scope("barrier"):
            pl.semaphore_wait(barrier, n - 1)

    @pl.when(jnp.logical_not(last))
    def _():
        send_near()

    @pl.when(outer_rest)
    def _():
        send(0, 0)
        send(0, 1)

    tail = blk_devs - 1
    spectra(1, 0)
    send(1, 0)
    spectra(2, 0)
    spectra(tail, 0)
    spectra(1, 1)
    spectra(2, 1)
    with jax.named_scope("plane"):
        arrived(near_in.at[pl.ds(0, freq_devs - 1)], near_recv)
        total = near_in[0].astype(jnp.float32)
        for f in range(1, freq_devs):
            total = total + near_in[f].astype(jnp.float32)
        plane_out[...] = total.astype(jnp.bfloat16)
        plane_ref[me_b] = plane_out[...]
    for offset in range(1, blk_devs):
        plane_copy(offset, me_b).start()
    recv_ref[me, 0] = outgoing[tail, me_f, 0]

    @pl.when(me_b < side)
    def _():
        send(tail, 0)
        send(2, 0)
        send(1, 1)
        send(2, 1)


    @pl.when(me_b == side)
    def _():
        send(2, 0, (0, 2))
        send(2, 1, (0, 2))
        send(2, 0, (2, freq_devs))
        send(2, 1, (2, freq_devs))
        send(tail, 0)
        send(1, 1)


    @pl.when(last)
    def _():
        send(tail, 0)
        send(1, 1)
        send(2, 0)

    for step in range(3, tail):
        for part in range(2):
            spectra(step, part)
            send(step, part)
    spectra(tail, 1)
    recv_ref[me, 1] = outgoing[tail, me_f, 1]
    send(tail, 1)
    with jax.named_scope("sort"):
        fill_sort(sort_ref, recv_ref.shape[2])
    with jax.named_scope("choice"):
        small[2].wait()
        fill_choice(freq_devs, packed, targets_ref, choose, pick, inside, fold, signs)

    @pl.when(last)
    def _():
        arrived(outgoing.at[0], send_sem.at[0])
        arrived(outgoing.at[1], send_sem.at[1])
        arrived(outgoing.at[2, :, 0], send_sem.at[2])
        send(2, 1)


    @pl.when(inner)
    def _():
        with jax.named_scope("forward"):
            forward(0)
            forward(1)

    with jax.named_scope("plane_wait"):
        arrived(plane_ref.at[pl.ds(0, blk_devs - 1)], plane_recv)
    with jax.named_scope("left"):
        fill_left(plane_ref, choose, pick, inside, fold, signs, left_ref)
    with jax.named_scope("first_part"):
        wait_part(0)
    with jax.named_scope("product"):
        for i in range(FREQ_DEV):
            rights = sorted_part(sort_ref, recv_ref, i, 0)
            for o in range(2):
                product(left_ref, rights, i, o, early_ref)
    with jax.named_scope("send_wait"):
        arrived(near_in.at[pl.ds(0, freq_devs - 1)], near_send)
        arrived(plane_ref.at[pl.ds(0, blk_devs - 1)], plane_send)

        @pl.when(jnp.logical_not(last))
        def _():
            for step in range(3):
                arrived(outgoing.at[step], send_sem.at[step])

        @pl.when(last)
        def _():
            arrived(outgoing.at[2, :, 1], send_sem.at[2])

        for step in range(3, blk_devs - 1):
            arrived(outgoing.at[step], send_sem.at[step])
        arrived(outgoing.at[blk_devs - 1, pl.ds(0, freq_devs - 1)], send_sem.at[blk_devs - 1])

        @pl.when(inner)
        def _():
            arrived(relay.at[pl.ds(0, freq_devs - 1)], relay_send)

    with jax.named_scope("recv_wait"):
        wait_part(1)


def sorted_part(sort_ref, recv_ref, i, part):
    shots, _, rows, lanes = recv_ref.shape
    lines = sort_ref[pl.ds(i * 4 * GROUP, 4 * GROUP), :]
    groups = []
    for g in range(shots // GROUP):
        received = recv_ref[pl.ds(g * GROUP, GROUP), part].reshape(GROUP * rows, lanes)
        groups.append(dot(lines, received).astype(jnp.bfloat16))
    halves = [slice(2 * GROUP * h, 2 * GROUP * (h + 1)) for h in range(2)]
    return [jnp.concatenate([r[half] for r in groups], 0) for half in halves]


def product(left_ref, rights, i, o, out_ref):
    count = left_ref.shape[1] // 2
    depth, lanes = rights[0].shape
    scale = 1.0 / math.sqrt(depth // 2)
    left = left_ref[i, pl.ds(o * count, count), :depth]
    for h, right in enumerate(rights):
        out_ref[i, pl.ds(o * count, count), pl.ds(h * lanes, lanes)] = dot(left, right) * scale


def fill_table(band_ref, fir_ref, table, freq_count):
    cols = table.shape[0] // 2
    time_count = table.shape[1]
    taps = fir_ref.shape[1]
    period = freq_count * time_count
    quarter = period // 4
    row = lax.broadcasted_iota(jnp.int32, (cols, taps), 0)
    time = lax.broadcasted_iota(jnp.int32, (cols, taps), 1)
    low = band_ref[0]
    high = band_ref[1]
    numerator = low * freq_count + (high - low) * (row >> 1)

    def cosine(turn):
        return cos_turns((turn & (period - 1)).astype(jnp.float32) * (1.0 / period))

    turn = numerator * time
    cos_in = cosine(turn)
    sin_in = cosine(turn + 3 * quarter)
    step = numerator * taps
    cos_step = cosine(step)
    sin_step = cosine(step + 3 * quarter)
    last = turn + numerator * (time_count - taps) + (row & 1) * quarter
    cos_last = cosine(last)
    sin_last = cosine(last + 3 * quarter)
    lag = lax.broadcasted_iota(jnp.int32, (taps, taps), 0)
    late = lax.broadcasted_iota(jnp.int32, (taps, taps), 1)
    kept = jnp.where(lag < taps - late, 1.0, 0.0).astype(jnp.float32)
    fir = fir_ref[...]
    weighted = jnp.concatenate([cos_in * fir, sin_in * fir], 0)
    sums = dot(weighted, kept, precision=lax.Precision.HIGHEST) * (1.0 / math.sqrt(time_count))
    sum_cos = sums[:cols]
    sum_sin = sums[cols:]
    odd = (row & 1) == 1
    cos_own = jnp.where(odd, -sin_in, cos_in)
    sin_own = jnp.where(odd, cos_in, sin_in)
    all_cos = jnp.broadcast_to(sum_cos[:, :1], (cols, taps))
    all_sin = jnp.broadcast_to(sum_sin[:, :1], (cols, taps))
    value = cos_own * all_cos - sin_own * all_sin
    other = sin_own * all_cos + cos_own * all_sin
    tiles = time_count // taps
    for tile in range(tiles):
        if tile == tiles - 1:
            value = cos_last * sum_cos - sin_last * sum_sin
        value_high = value.astype(jnp.bfloat16)
        value_low = (value - value_high.astype(jnp.float32)).astype(jnp.bfloat16)
        table[pl.ds(0, cols), pl.ds(tile * taps, taps)] = value_high
        table[pl.ds(cols, cols), pl.ds(tile * taps, taps)] = value_low
        if tile < tiles - 2:
            value, other = (
                value * cos_step - other * sin_step,
                other * cos_step + value * sin_step,
            )


def fill_sort(sort_ref, rows):
    lines, depth = sort_ref.shape
    half = rows // 2
    line = lax.broadcasted_iota(jnp.int32, (lines, depth), 0)
    place = lax.broadcasted_iota(jnp.int32, (lines, depth), 1)
    group = line // GROUP
    home = (line % GROUP) * rows + (group // 2) % 2 * half + group // 4 * 2 + group % 2
    sort_ref[...] = jnp.where(place == home, 1.0, 0.0).astype(jnp.bfloat16)


def fill_choice(freq_devs, packed, targets_ref, choose, pick, inside, fold, signs):
    count = targets_ref.shape[1]
    shots = choose.shape[1] // 2
    lines, depth = pick.shape
    near_lanes, wide = fold.shape
    near_rows = freq_devs // packed * PARTS
    wanted = jnp.broadcast_to(targets_ref[...].astype(jnp.float32), (128, count)).T
    shot = lax.broadcasted_iota(jnp.int32, (count, 2 * shots), 1) % shots
    choose[...] = jnp.where(shot == wanted[:, :1].astype(jnp.int32), 1.0, 0.0).astype(jnp.bfloat16)

    taken = lines if shots <= 64 else shots
    for first in range(0, lines, taken):
        line = lax.broadcasted_iota(jnp.int32, (taken, depth), 0) + first
        place = lax.broadcasted_iota(jnp.int32, (taken, depth), 1)
        part = line // shots
        from_shot = line % shots
        from_f = from_shot % freq_devs
        home = (from_shot // freq_devs) * near_rows + (from_f // packed) * PARTS + part
        pick[pl.ds(first, taken), :] = jnp.where(place == home, 1.0, 0.0).astype(jnp.bfloat16)

    line = lax.broadcasted_iota(jnp.int32, (lines, near_lanes), 0)
    lane = lax.broadcasted_iota(jnp.int32, (lines, near_lanes), 1)
    slot = line % shots % freq_devs % packed
    inside[...] = jnp.where(lane // shots == slot, 1.0, 0.0)

    row = lax.broadcasted_iota(jnp.int32, (near_lanes, wide), 0)
    lane = lax.broadcasted_iota(jnp.int32, (near_lanes, wide), 1)
    spot = lane // (2 * GROUP) * GROUP + lane % GROUP
    fold[...] = jnp.where(row % shots == spot % shots, 1.0, 0.0).astype(jnp.bfloat16)

    source = lax.broadcasted_iota(jnp.int32, (2 * shots, wide), 0) // shots
    lane = lax.broadcasted_iota(jnp.int32, (2 * shots, wide), 1)
    target = lane // GROUP % 2
    used = jnp.where(lane < 2 * shots, 1.0, 0.0)
    signs[0] = jnp.where(source == target, jnp.where(source == 1, -used, used), 0.0)
    signs[1] = jnp.where(source == target, 0.0, used)


def fill_left(plane_ref, choose, pick, inside, fold, signs, left_ref):
    blk_devs, near_rows, near_lanes = plane_ref.shape
    count, depth = choose.shape
    wide = fold.shape[1]
    batch = FREQ_DEV if depth <= 128 else 1
    planes = plane_ref[...].reshape(blk_devs * near_rows, near_lanes)
    for first in range(0, FREQ_DEV, batch):
        lines = pl.ds(first * depth, batch * depth)
        near = (dot(pick[lines, :], planes) * inside[lines, :]).astype(jnp.bfloat16)
        near = dot(near, fold[...])
        parts = []
        for i in range(batch):
            for o in range(2):
                parts.append((near[i * depth : (i + 1) * depth] * signs[o]).astype(jnp.bfloat16))
        lefts = dot(choose[...], jnp.concatenate(parts, 1)).astype(jnp.bfloat16)
        for k in range(2 * batch):
            o = k % 2
            rows = pl.ds(o * count, count)
            left_ref[first + k // 2, rows, :] = lefts[:, k * wide : (k + 1) * wide]


def product_kernel(early_ref, recv_ref, left_ref, sort_ref, out_ref, made, sems):
    half = made.shape[2]
    count = made.shape[1] // 2

    def write(source, i, o, part):
        return pltpu.make_async_copy(
            source.at[i, pl.ds(o * count, count)],
            out_ref.at[i, o, :, pl.ds(part * half, half)],
            sems.at[part, i, o],
        )

    for i in range(FREQ_DEV):
        for o in range(2):
            write(early_ref, i, o, 0).start()
    for i in range(FREQ_DEV):
        rights = sorted_part(sort_ref, recv_ref, i, 1)
        for o in range(2):
            product(left_ref, rights, i, o, made)
            write(made, i, o, 1).start()

    for part, source in enumerate((early_ref, made)):
        for i in range(FREQ_DEV):
            for o in range(2):
                write(source, i, o, part).wait()


def per_device(traces, fir, targets, band):
    shot_dev, rec_count, time_count = traces.shape
    freq_devs = lax.axis_size("freq")
    blk_devs = lax.axis_size("blk")
    n = freq_devs * blk_devs
    assert shot_dev == 1
    assert blk_devs & (blk_devs - 1) == 0
    col_stride = rec_count // n
    width = rec_count // blk_devs
    lanes = width // 4
    near_lanes = max(128, n)
    packed = near_lanes // n
    near_rows = freq_devs // packed * PARTS
    cols = 2 * FREQ_DEV * freq_devs
    count = targets.shape[0]
    assert n % GROUP == 0
    limit = VMEM_LIMIT if n <= 64 else VMEM_LARGE
    lines = 4 * FREQ_DEV * GROUP
    wide = max(128, 2 * n)
    hbm = lambda x: pltpu.with_memory_space_constraint(x, pltpu.HBM)
    received, lefts, sorter, early = pl.pallas_call(
        functools.partial(send_kernel, freq_devs, blk_devs, col_stride),
        out_shape=[
            pltpu.VMEM((n, 2, ROWS, lanes), jnp.bfloat16),
            pltpu.VMEM((FREQ_DEV, 2 * count, wide), jnp.bfloat16),
            pltpu.VMEM((lines, GROUP * ROWS), jnp.bfloat16),
            pltpu.VMEM((FREQ_DEV, 2 * count, width // 2), jnp.float32),
        ],
        in_specs=[pl.BlockSpec(memory_space=pl.ANY)] * 4,
        out_specs=[pl.BlockSpec(memory_space=pltpu.VMEM)] * 4,
        scratch_shapes=[
            pltpu.SMEM((2,), jnp.int32),
            pltpu.VMEM((1, fir.shape[0]), jnp.float32),
            pltpu.VMEM((1, count), jnp.int32),
            pltpu.VMEM((n, col_stride, time_count), jnp.bfloat16),
            pltpu.VMEM((n, 16, time_count), jnp.bfloat16),
            pltpu.VMEM((2 * cols, time_count), jnp.bfloat16),
            pltpu.VMEM((blk_devs, freq_devs, 2, ROWS, lanes), jnp.bfloat16),
            pltpu.VMEM((freq_devs, 2, ROWS, lanes), jnp.bfloat16),
            pltpu.VMEM((freq_devs, near_rows, near_lanes), jnp.bfloat16),
            pltpu.VMEM((freq_devs, near_rows, near_lanes), jnp.bfloat16),
            pltpu.VMEM((near_rows, near_lanes), jnp.bfloat16),
            pltpu.VMEM((blk_devs, near_rows, near_lanes), jnp.bfloat16),
            pltpu.VMEM((count, 2 * n), jnp.bfloat16),
            pltpu.VMEM((FREQ_DEV * 2 * n, blk_devs * near_rows), jnp.bfloat16),
            pltpu.VMEM((FREQ_DEV * 2 * n, near_lanes), jnp.float32),
            pltpu.VMEM((near_lanes, wide), jnp.bfloat16),
            pltpu.VMEM((2, 2 * n, wide), jnp.float32),
            pltpu.SemaphoreType.DMA((3,)),
            pltpu.SemaphoreType.DMA((blk_devs, 2)),
            pltpu.SemaphoreType.DMA,
            pltpu.SemaphoreType.DMA((blk_devs,)),
            pltpu.SemaphoreType.DMA((2,)),
            pltpu.SemaphoreType.DMA,
            pltpu.SemaphoreType.DMA,
            pltpu.SemaphoreType.DMA,
            pltpu.SemaphoreType.DMA,
            pltpu.SemaphoreType.DMA,
            pltpu.SemaphoreType.DMA((2,)),
            pltpu.SemaphoreType.REGULAR,
        ],
        compiler_params=pltpu.CompilerParams(
            collective_id=0, has_side_effects=True, vmem_limit_bytes=limit
        ),
    )(
        hbm(band),
        hbm(fir.reshape(1, -1)),
        hbm(targets.reshape(1, -1)),
        hbm(traces.reshape(n, col_stride, time_count)),
    )
    return pl.pallas_call(
        product_kernel,
        out_shape=jax.ShapeDtypeStruct((FREQ_DEV, 2, count, width), jnp.float32),
        in_specs=[pl.BlockSpec(memory_space=pltpu.VMEM)] * 4,
        out_specs=pl.BlockSpec(memory_space=pl.ANY),
        scratch_shapes=[
            pltpu.VMEM((FREQ_DEV, 2 * count, width // 2), jnp.float32),
            pltpu.SemaphoreType.DMA((2, FREQ_DEV, 2)),
        ],
        compiler_params=pltpu.CompilerParams(vmem_limit_bytes=limit),
    )(early, received, lefts, sorter)


def solution(mesh):
    placed = (P(("blk", "freq"), None, None), P(), P(), P())
    return jax.shard_map(
        per_device,
        mesh=mesh,
        in_specs=placed,
        out_specs=P("freq", None, None, "blk"),
        check_vma=False,
    )
```

```python
import functools
import math

import jax
import jax.numpy as jnp
from jax import lax
from jax.experimental import pallas as pl
from jax.experimental.pallas import tpu as pltpu
from jax.sharding import PartitionSpec as P

FREQ_DEV = 4
PARTS = 2 * FREQ_DEV
ROWS = 2 * PARTS
VMEM_LIMIT = 40 * 2**20
VMEM_LARGE = 52 * 2**20
GROUP = 32
UNROLL = True
EARLY = 2
MESH = pl.DeviceIdType.MESH


def dot(a, b, dims=(((1,), (0,)), ((), ())), precision=None):
    return lax.dot_general(a, b, dims, precision=precision, preferred_element_type=jnp.float32)


def cos_turns(turns):
    w = (0.25 - jnp.abs(turns - 0.5)) * (2.0 * math.pi)
    w2 = w * w
    total = jnp.full_like(w, 1.0 / math.factorial(13))
    for order in (11, 9, 7, 5, 3, 1):
        sign = 1.0 if order % 4 == 1 else -1.0
        total = total * w2 + sign / math.factorial(order)
    return -(total * w)


def flipped(index, offset, count):
    total = 0
    bit = 1
    while bit < count:
        total = total + bit * lax.rem(index // bit + (offset // bit) % 2, 2)
        bit *= 2
    return total


def send_kernel(
    freq_devs, blk_devs, col_stride,
    band_hbm, fir_hbm, targets_hbm, traces_ref, recv_ref, left_ref, sort_ref, early_ref,
    band_ref, fir_ref, targets_ref,
    traces_buf, spots_buf, table, outgoing, relay, near_out, near_in, plane_out, plane_ref,
    choose, pick, inside, fold, signs,
    small_sem, chunk_sem, spot_sem, send_sem, recv_sem,
    near_send, near_recv, plane_send, plane_recv, relay_send, relay_recv, go,
):
    me_f = lax.axis_index("freq")
    me_b = lax.axis_index("blk")
    me = me_b * freq_devs + me_f
    n = freq_devs * blk_devs
    spots, _, time_count = traces_buf.shape
    rec_count = spots * col_stride
    width = rec_count // blk_devs
    lanes = width // 4
    freq_count = FREQ_DEV * freq_devs
    cols = 2 * freq_count
    per = width // col_stride
    _, near_rows, near_lanes = near_out.shape
    packed = near_lanes // spots

    side = blk_devs // 2
    high = me_b // side
    depth = (1 - high) * (side - 1 - me_b) + high * (me_b - side)
    mate_b = blk_devs - 1 - me_b
    mate = mate_b * freq_devs + me_f
    inner = depth == 0
    last = me_b == blk_devs - 1
    ranks = [lax.rem(depth + step, side) for step in range(side)]
    blocks = [(1 - high) * (side + r) + high * (side - 1 - r) for r in ranks]
    blocks += [high * side + lax.rem(me_b + 1 + step, side) for step in range(side)]
    late = (me_b // side)
    delayed = blocks[1]
    blocks[1] = (1 - late) * delayed + late * blocks[side]
    blocks[side] = (1 - late) * blocks[side] + late * delayed
    piece = per // 2

    def spot_copy():
        return pltpu.make_async_copy(
            traces_ref.at[:, pl.ds(0, 16), :], spots_buf, spot_sem
        )

    def chunk_copy(step, part):
        return pltpu.make_async_copy(
            traces_ref.at[pl.ds(blocks[step] * per + part * piece, piece)],
            traces_buf.at[pl.ds(step * per + part * piece, piece)],
            chunk_sem.at[step, part],
        )

    def signal(f, block, sem):
        pl.semaphore_signal(sem, inc=1, device_id=(f, block), device_id_type=MESH)

    def signal_block(block, first):
        @pl.loop(first, freq_devs, unroll=UNROLL)
        def _(d):
            signal(lax.rem(me_f + d, freq_devs), block, barrier)

    def announce():
        @pl.when(inner)
        def _():
            signal(me_f, mate_b, barrier)

        for block in range(blk_devs - 1, -1, -1):
            if block not in (side - 1, side):

                @pl.when(me_b == block)
                def _():
                    signal_block(block, 1)

                @pl.when(me_b != block)
                def _():
                    signal_block(block, 0)

    def near_copy(f):
        return pltpu.make_async_remote_copy(
            src_ref=near_out.at[f],
            dst_ref=near_in.at[me_f],
            send_sem=near_send,
            recv_sem=near_recv,
            device_id=(f, me_b),
            device_id_type=MESH,
        )

    def plane_copy(offset, slot):
        return pltpu.make_async_remote_copy(
            src_ref=plane_out,
            dst_ref=plane_ref.at[slot],
            send_sem=plane_send,
            recv_sem=plane_recv,
            device_id=(me_f, flipped(me_b, offset, blk_devs)),
            device_id_type=MESH,
        )

    def send(step, part, some=None):
        first = 1 if step == blk_devs - 1 else 0
        turn = me_f if first else me_f * (blocks[step] // side)

        start, stop = some or (first, freq_devs)

        @pl.loop(start, stop, unroll=UNROLL)
        def _(d):
            f = lax.rem(turn + d, freq_devs)
            pltpu.make_async_remote_copy(
                src_ref=outgoing.at[step, f, part],
                dst_ref=recv_ref.at[me, part],
                send_sem=send_sem.at[step],
                recv_sem=recv_sem.at[part],
                device_id=(f, blocks[step]),
                device_id_type=MESH,
            ).start()

    def relay_copy(part):
        return pltpu.make_async_remote_copy(
            src_ref=outgoing.at[0, :, pl.ds(part, 1)],
            dst_ref=relay.at[:, pl.ds(part, 1)],
            send_sem=send_sem.at[0],
            recv_sem=relay_recv.at[part],
            device_id=(me_f, mate_b),
            device_id_type=MESH,
        )

    def forward(part):
        relay_copy(part).wait_recv()
        recv_ref[mate, part] = relay[me_f, part]

        @pl.loop(1, freq_devs, unroll=UNROLL)
        def _(d):
            f = lax.rem(me_f + d, freq_devs)
            pltpu.make_async_remote_copy(
                src_ref=relay.at[f, part],
                dst_ref=recv_ref.at[mate, part],
                send_sem=relay_send,
                recv_sem=recv_sem.at[part],
                device_id=(f, me_b),
                device_id_type=MESH,
            ).start()

    def wait_part(part):
        @pl.when(inner)
        def _():
            arrived(recv_ref.at[pl.ds(0, n - 2), part], recv_sem.at[part])

        @pl.when(jnp.logical_not(inner))
        def _():
            arrived(recv_ref.at[pl.ds(0, n - 1), part], recv_sem.at[part])

    def arrived(ref, sem):
        pltpu.make_async_copy(ref, ref, sem).wait()

    small = [
        pltpu.make_async_copy(band_hbm, band_ref, small_sem.at[0]),
        pltpu.make_async_copy(fir_hbm, fir_ref, small_sem.at[1]),
        pltpu.make_async_copy(targets_hbm, targets_ref, small_sem.at[2]),
    ]
    barrier = pltpu.get_barrier_semaphore()
    small[0].start()
    small[1].start()
    chunk_copy(0, 0).start()
    with jax.named_scope("signals"):
        announce()
    spot_copy().start()
    with jax.named_scope("small_wait"):
        small[0].wait()
        small[1].wait()
    chunk_copy(0, 1).start()
    with jax.named_scope("table"):
        fill_table(band_ref, fir_ref, table, freq_count)

    def spectrum_of(rows):
        both = dot(table[...], rows, (((1,), (1,)), ((), ())))
        return both[:cols] + both[cols:]

    def spectra(step, part):
        with jax.named_scope(f"chunk{step}{part}"):
            chunk_copy(step, part).wait()
            rows = traces_buf[pl.ds(step * per + part * piece, piece)]
            values = spectrum_of(rows.reshape(2 * lanes, time_count))
            values = values.reshape(freq_devs, PARTS, 2 * lanes)
            values = jnp.concatenate([values[:, :, :lanes], values[:, :, lanes:]], 1)
            outgoing[step, :, part] = values.astype(jnp.bfloat16)

    chunk_copy(1, 0).start()
    small[2].start()
    def spots_near():
        with jax.named_scope("spots"):
            spot_copy().wait()
            shift = lax.rem(me_f, packed) * spots
            taken = min(spots, 64)
            at_spots = None
            for first in range(0, spots, taken):
                rows = spots_buf[pl.ds(first, taken)].reshape(taken * 16, time_count)
                near = spectrum_of(rows).astype(jnp.bfloat16)
                spot_row = lax.broadcasted_iota(jnp.int32, (taken * 16, near_lanes), 0)
                spot_col = lax.broadcasted_iota(jnp.int32, (taken * 16, near_lanes), 1)
                here = spot_row == (spot_col - shift - first) * 16
                some = dot(near, jnp.where(here, 1.0, 0.0).astype(jnp.bfloat16))
                at_spots = some if at_spots is None else at_spots + some
            at_spots = at_spots.reshape(freq_devs, PARTS, near_lanes)
            at_spots = jnp.concatenate([at_spots] * 2, 1)
            line = lax.broadcasted_iota(jnp.int32, at_spots.shape, 1) // PARTS
            for pair in range(near_rows // (2 * PARTS)):
                kept = jnp.where(line + 2 * pair == me_f // packed, at_spots, 0.0)
                near_out[:, pl.ds(2 * PARTS * pair, 2 * PARTS), :] = kept.astype(jnp.bfloat16)
            near_in[me_f] = near_out[me_f]

    def send_near():

        @pl.loop(1, freq_devs, unroll=UNROLL)
        def _(d):
            near_copy(lax.rem(me_f + d, freq_devs)).start()

    @pl.when(last)
    def _():
        with jax.named_scope("barrier"):
            pl.semaphore_wait(barrier, n - 1)
        signal(me_f, side, go)
        signal(me_f, side - 1, go)
        spots_near()
        send_near()

    for part in range(2):
        spectra(0, part)

        @pl.when(inner)
        def _():
            if part == 0:
                with jax.named_scope("mate"):
                    pl.semaphore_wait(barrier, 1)
            relay_copy(part).start()

        @pl.when(last)
        def _():
            send(0, part)

        if part == 0:
            chunk_copy(1, 1).start()
            for step in range(2, blk_devs):
                chunk_copy(step, 0).start()
                chunk_copy(step, 1).start()

    outer_rest = jnp.logical_not(jnp.logical_or(inner, last))

    @pl.when(jnp.logical_not(last))
    def _():
        spots_near()

    @pl.when(inner)
    def _():
        with jax.named_scope("go"):
            pl.semaphore_wait(go, 1)

    @pl.when(outer_rest)
    def _():
        with jax.named_scope("barrier"):
            pl.semaphore_wait(barrier, n - 1)

    @pl.when(jnp.logical_not(last))
    def _():
        send_near()

    @pl.when(outer_rest)
    def _():
        send(0, 0)
        send(0, 1)

    tail = blk_devs - 1
    spectra(1, 0)
    send(1, 0)
    spectra(2, 0)
    spectra(tail, 0)
    spectra(1, 1)
    spectra(2, 1)
    with jax.named_scope("plane"):
        arrived(near_in.at[pl.ds(0, freq_devs - 1)], near_recv)
        total = near_in[0].astype(jnp.float32)
        for f in range(1, freq_devs):
            total = total + near_in[f].astype(jnp.float32)
        plane_out[...] = total.astype(jnp.bfloat16)
        plane_ref[me_b] = plane_out[...]
    for offset in range(1, blk_devs):
        plane_copy(offset, me_b).start()
    recv_ref[me, 0] = outgoing[tail, me_f, 0]

    @pl.when(me_b < side)
    def _():
        send(2, 0, (0, 2))
        send(2, 1, (0, 2))
        send(2, 0, (2, freq_devs))
        send(2, 1, (2, freq_devs))
        send(tail, 0)
        send(1, 1)


    @pl.when(me_b == side)
    def _():
        send(1, 1)
        send(2, 0, (0, 2))
        send(2, 1, (0, 2))
        send(2, 0, (2, freq_devs))
        send(2, 1, (2, freq_devs))
        send(tail, 0)


    @pl.when(last)
    def _():
        send(tail, 0)
        send(1, 1)

    for step in range(3, tail):
        for part in range(2):
            spectra(step, part)
            send(step, part)
    spectra(tail, 1)
    recv_ref[me, 1] = outgoing[tail, me_f, 1]
    send(tail, 1)
    with jax.named_scope("sort"):
        fill_sort(sort_ref, recv_ref.shape[2])
    with jax.named_scope("choice"):
        small[2].wait()
        fill_choice(freq_devs, packed, targets_ref, choose, pick, inside, fold, signs)

    @pl.when(last)
    def _():
        arrived(outgoing.at[0], send_sem.at[0])
        arrived(outgoing.at[1], send_sem.at[1])
        send(2, 0)
        arrived(outgoing.at[2, :, 0], send_sem.at[2])
        send(2, 1)


    @pl.when(inner)
    def _():
        with jax.named_scope("forward"):
            forward(0)
            forward(1)

    with jax.named_scope("plane_wait"):
        arrived(plane_ref.at[pl.ds(0, blk_devs - 1)], plane_recv)
    with jax.named_scope("left"):
        fill_left(plane_ref, choose, pick, inside, fold, signs, left_ref)
    with jax.named_scope("first_part"):
        wait_part(0)
    with jax.named_scope("product"):
        for i in range(EARLY):
            rights = sorted_part(sort_ref, recv_ref, i, 0)
            for o in range(2):
                product(left_ref, rights, i, o, early_ref.at[i])
    with jax.named_scope("send_wait"):
        arrived(near_in.at[pl.ds(0, freq_devs - 1)], near_send)
        arrived(plane_ref.at[pl.ds(0, blk_devs - 1)], plane_send)

        @pl.when(jnp.logical_not(last))
        def _():
            for step in range(3):
                arrived(outgoing.at[step], send_sem.at[step])

        @pl.when(last)
        def _():
            arrived(outgoing.at[2, :, 1], send_sem.at[2])

        for step in range(3, blk_devs - 1):
            arrived(outgoing.at[step], send_sem.at[step])
        arrived(outgoing.at[blk_devs - 1, pl.ds(0, freq_devs - 1)], send_sem.at[blk_devs - 1])

        @pl.when(inner)
        def _():
            arrived(relay.at[pl.ds(0, freq_devs - 1)], relay_send)

    with jax.named_scope("recv_wait"):
        wait_part(1)


def sorted_part(sort_ref, recv_ref, i, part):
    shots, _, rows, lanes = recv_ref.shape
    lines = sort_ref[pl.ds(i * 4 * GROUP, 4 * GROUP), :]
    groups = []
    for g in range(shots // GROUP):
        received = recv_ref[pl.ds(g * GROUP, GROUP), part].reshape(GROUP * rows, lanes)
        groups.append(dot(lines, received).astype(jnp.bfloat16))
    halves = [slice(2 * GROUP * h, 2 * GROUP * (h + 1)) for h in range(2)]
    return [jnp.concatenate([r[half] for r in groups], 0) for half in halves]


def product(left_ref, rights, i, o, out_ref):
    count = left_ref.shape[1] // 2
    depth, lanes = rights[0].shape
    scale = 1.0 / math.sqrt(depth // 2)
    left = left_ref[i, pl.ds(o * count, count), :depth]
    for h, right in enumerate(rights):
        out_ref[pl.ds(o * count, count), pl.ds(h * lanes, lanes)] = dot(left, right) * scale


def fill_table(band_ref, fir_ref, table, freq_count):
    cols = table.shape[0] // 2
    time_count = table.shape[1]
    taps = fir_ref.shape[1]
    period = freq_count * time_count
    quarter = period // 4
    row = lax.broadcasted_iota(jnp.int32, (cols, taps), 0)
    time = lax.broadcasted_iota(jnp.int32, (cols, taps), 1)
    low = band_ref[0]
    high = band_ref[1]
    numerator = low * freq_count + (high - low) * (row >> 1)

    def cosine(turn):
        return cos_turns((turn & (period - 1)).astype(jnp.float32) * (1.0 / period))

    turn = numerator * time
    cos_in = cosine(turn)
    sin_in = cosine(turn + 3 * quarter)
    step = numerator * taps
    cos_step = cosine(step)
    sin_step = cosine(step + 3 * quarter)
    last = turn + numerator * (time_count - taps) + (row & 1) * quarter
    cos_last = cosine(last)
    sin_last = cosine(last + 3 * quarter)
    lag = lax.broadcasted_iota(jnp.int32, (taps, taps), 0)
    late = lax.broadcasted_iota(jnp.int32, (taps, taps), 1)
    kept = jnp.where(lag < taps - late, 1.0, 0.0).astype(jnp.float32)
    fir = fir_ref[...]
    weighted = jnp.concatenate([cos_in * fir, sin_in * fir], 0)
    sums = dot(weighted, kept, precision=lax.Precision.HIGHEST) * (1.0 / math.sqrt(time_count))
    sum_cos = sums[:cols]
    sum_sin = sums[cols:]
    odd = (row & 1) == 1
    cos_own = jnp.where(odd, -sin_in, cos_in)
    sin_own = jnp.where(odd, cos_in, sin_in)
    all_cos = jnp.broadcast_to(sum_cos[:, :1], (cols, taps))
    all_sin = jnp.broadcast_to(sum_sin[:, :1], (cols, taps))
    value = cos_own * all_cos - sin_own * all_sin
    other = sin_own * all_cos + cos_own * all_sin
    tiles = time_count // taps
    for tile in range(tiles):
        if tile == tiles - 1:
            value = cos_last * sum_cos - sin_last * sum_sin
        value_high = value.astype(jnp.bfloat16)
        value_low = (value - value_high.astype(jnp.float32)).astype(jnp.bfloat16)
        table[pl.ds(0, cols), pl.ds(tile * taps, taps)] = value_high
        table[pl.ds(cols, cols), pl.ds(tile * taps, taps)] = value_low
        if tile < tiles - 2:
            value, other = (
                value * cos_step - other * sin_step,
                other * cos_step + value * sin_step,
            )


def fill_sort(sort_ref, rows):
    lines, depth = sort_ref.shape
    half = rows // 2
    line = lax.broadcasted_iota(jnp.int32, (lines, depth), 0)
    place = lax.broadcasted_iota(jnp.int32, (lines, depth), 1)
    group = line // GROUP
    home = (line % GROUP) * rows + (group // 2) % 2 * half + group // 4 * 2 + group % 2
    sort_ref[...] = jnp.where(place == home, 1.0, 0.0).astype(jnp.bfloat16)


def fill_choice(freq_devs, packed, targets_ref, choose, pick, inside, fold, signs):
    count = targets_ref.shape[1]
    shots = choose.shape[1] // 2
    lines, depth = pick.shape
    near_lanes, wide = fold.shape
    near_rows = freq_devs // packed * PARTS
    wanted = jnp.broadcast_to(targets_ref[...].astype(jnp.float32), (128, count)).T
    shot = lax.broadcasted_iota(jnp.int32, (count, 2 * shots), 1) % shots
    choose[...] = jnp.where(shot == wanted[:, :1].astype(jnp.int32), 1.0, 0.0).astype(jnp.bfloat16)

    taken = lines if shots <= 64 else shots
    for first in range(0, lines, taken):
        line = lax.broadcasted_iota(jnp.int32, (taken, depth), 0) + first
        place = lax.broadcasted_iota(jnp.int32, (taken, depth), 1)
        part = line // shots
        from_shot = line % shots
        from_f = from_shot % freq_devs
        home = (from_shot // freq_devs) * near_rows + (from_f // packed) * PARTS + part
        pick[pl.ds(first, taken), :] = jnp.where(place == home, 1.0, 0.0).astype(jnp.bfloat16)

    line = lax.broadcasted_iota(jnp.int32, (lines, near_lanes), 0)
    lane = lax.broadcasted_iota(jnp.int32, (lines, near_lanes), 1)
    slot = line % shots % freq_devs % packed
    inside[...] = jnp.where(lane // shots == slot, 1.0, 0.0)

    row = lax.broadcasted_iota(jnp.int32, (near_lanes, wide), 0)
    lane = lax.broadcasted_iota(jnp.int32, (near_lanes, wide), 1)
    spot = lane // (2 * GROUP) * GROUP + lane % GROUP
    fold[...] = jnp.where(row % shots == spot % shots, 1.0, 0.0).astype(jnp.bfloat16)

    source = lax.broadcasted_iota(jnp.int32, (2 * shots, wide), 0) // shots
    lane = lax.broadcasted_iota(jnp.int32, (2 * shots, wide), 1)
    target = lane // GROUP % 2
    used = jnp.where(lane < 2 * shots, 1.0, 0.0)
    signs[0] = jnp.where(source == target, jnp.where(source == 1, -used, used), 0.0)
    signs[1] = jnp.where(source == target, 0.0, used)


def fill_left(plane_ref, choose, pick, inside, fold, signs, left_ref):
    blk_devs, near_rows, near_lanes = plane_ref.shape
    count, depth = choose.shape
    wide = fold.shape[1]
    batch = FREQ_DEV if depth <= 128 else 1
    planes = plane_ref[...].reshape(blk_devs * near_rows, near_lanes)
    for first in range(0, FREQ_DEV, batch):
        lines = pl.ds(first * depth, batch * depth)
        near = (dot(pick[lines, :], planes) * inside[lines, :]).astype(jnp.bfloat16)
        near = dot(near, fold[...])
        parts = []
        for i in range(batch):
            for o in range(2):
                parts.append((near[i * depth : (i + 1) * depth] * signs[o]).astype(jnp.bfloat16))
        lefts = dot(choose[...], jnp.concatenate(parts, 1)).astype(jnp.bfloat16)
        for k in range(2 * batch):
            o = k % 2
            rows = pl.ds(o * count, count)
            left_ref[first + k // 2, rows, :] = lefts[:, k * wide : (k + 1) * wide]


def product_kernel(early_ref, recv_ref, left_ref, sort_ref, out_ref, made, sems):
    half = made.shape[3]
    count = made.shape[2] // 2

    def write(source, i, o, part):
        return pltpu.make_async_copy(
            source.at[pl.ds(o * count, count)],
            out_ref.at[i, o, :, pl.ds(part * half, half)],
            sems.at[part, i, o],
        )

    def source(i, part):
        return early_ref.at[i] if part == 0 and i < EARLY else made.at[part, i]

    for i in range(EARLY):
        for o in range(2):
            write(source(i, 0), i, o, 0).start()
    for i in range(FREQ_DEV):
        for part in range(2):
            if part or i >= EARLY:
                rights = sorted_part(sort_ref, recv_ref, i, part)
                for o in range(2):
                    product(left_ref, rights, i, o, made.at[part, i])
                    write(made.at[part, i], i, o, part).start()

    for i in range(FREQ_DEV):
        for part in range(2):
            for o in range(2):
                write(source(i, part), i, o, part).wait()


def per_device(traces, fir, targets, band):
    shot_dev, rec_count, time_count = traces.shape
    freq_devs = lax.axis_size("freq")
    blk_devs = lax.axis_size("blk")
    n = freq_devs * blk_devs
    assert shot_dev == 1
    assert blk_devs & (blk_devs - 1) == 0
    col_stride = rec_count // n
    width = rec_count // blk_devs
    lanes = width // 4
    near_lanes = max(128, n)
    packed = near_lanes // n
    near_rows = freq_devs // packed * PARTS
    cols = 2 * FREQ_DEV * freq_devs
    count = targets.shape[0]
    assert n % GROUP == 0
    limit = VMEM_LIMIT if n <= 64 else VMEM_LARGE
    lines = 4 * FREQ_DEV * GROUP
    wide = max(128, 2 * n)
    hbm = lambda x: pltpu.with_memory_space_constraint(x, pltpu.HBM)
    received, lefts, sorter, early = pl.pallas_call(
        functools.partial(send_kernel, freq_devs, blk_devs, col_stride),
        out_shape=[
            pltpu.VMEM((n, 2, ROWS, lanes), jnp.bfloat16),
            pltpu.VMEM((FREQ_DEV, 2 * count, wide), jnp.bfloat16),
            pltpu.VMEM((lines, GROUP * ROWS), jnp.bfloat16),
            pltpu.VMEM((EARLY, 2 * count, width // 2), jnp.float32),
        ],
        in_specs=[pl.BlockSpec(memory_space=pl.ANY)] * 4,
        out_specs=[pl.BlockSpec(memory_space=pltpu.VMEM)] * 4,
        scratch_shapes=[
            pltpu.SMEM((2,), jnp.int32),
            pltpu.VMEM((1, fir.shape[0]), jnp.float32),
            pltpu.VMEM((1, count), jnp.int32),
            pltpu.VMEM((n, col_stride, time_count), jnp.bfloat16),
            pltpu.VMEM((n, 16, time_count), jnp.bfloat16),
            pltpu.VMEM((2 * cols, time_count), jnp.bfloat16),
            pltpu.VMEM((blk_devs, freq_devs, 2, ROWS, lanes), jnp.bfloat16),
            pltpu.VMEM((freq_devs, 2, ROWS, lanes), jnp.bfloat16),
            pltpu.VMEM((freq_devs, near_rows, near_lanes), jnp.bfloat16),
            pltpu.VMEM((freq_devs, near_rows, near_lanes), jnp.bfloat16),
            pltpu.VMEM((near_rows, near_lanes), jnp.bfloat16),
            pltpu.VMEM((blk_devs, near_rows, near_lanes), jnp.bfloat16),
            pltpu.VMEM((count, 2 * n), jnp.bfloat16),
            pltpu.VMEM((FREQ_DEV * 2 * n, blk_devs * near_rows), jnp.bfloat16),
            pltpu.VMEM((FREQ_DEV * 2 * n, near_lanes), jnp.float32),
            pltpu.VMEM((near_lanes, wide), jnp.bfloat16),
            pltpu.VMEM((2, 2 * n, wide), jnp.float32),
            pltpu.SemaphoreType.DMA((3,)),
            pltpu.SemaphoreType.DMA((blk_devs, 2)),
            pltpu.SemaphoreType.DMA,
            pltpu.SemaphoreType.DMA((blk_devs,)),
            pltpu.SemaphoreType.DMA((2,)),
            pltpu.SemaphoreType.DMA,
            pltpu.SemaphoreType.DMA,
            pltpu.SemaphoreType.DMA,
            pltpu.SemaphoreType.DMA,
            pltpu.SemaphoreType.DMA,
            pltpu.SemaphoreType.DMA((2,)),
            pltpu.SemaphoreType.REGULAR,
        ],
        compiler_params=pltpu.CompilerParams(
            collective_id=0, has_side_effects=True, vmem_limit_bytes=limit
        ),
    )(
        hbm(band),
        hbm(fir.reshape(1, -1)),
        hbm(targets.reshape(1, -1)),
        hbm(traces.reshape(n, col_stride, time_count)),
    )
    return pl.pallas_call(
        product_kernel,
        out_shape=jax.ShapeDtypeStruct((FREQ_DEV, 2, count, width), jnp.float32),
        in_specs=[pl.BlockSpec(memory_space=pltpu.VMEM)] * 4,
        out_specs=pl.BlockSpec(memory_space=pl.ANY),
        scratch_shapes=[
            pltpu.VMEM((2, FREQ_DEV, 2 * count, width // 2), jnp.float32),
            pltpu.SemaphoreType.DMA((2, FREQ_DEV, 2)),
        ],
        compiler_params=pltpu.CompilerParams(vmem_limit_bytes=limit),
    )(early, received, lefts, sorter)


def solution(mesh):
    placed = (P(("blk", "freq"), None, None), P(), P(), P())
    return jax.shard_map(
        per_device,
        mesh=mesh,
        in_specs=placed,
        out_specs=P("freq", None, None, "blk"),
        check_vma=False,
    )
```
